512 devices in a mesh: cd: 64 (over z, y_lo, core), ab: 8 (over y_hi, x).
Axes of the slice: x: 4, y: 4 (y_hi: 2, y_lo: 2; y = y_hi * 2 + y_lo), z: 16, core: 2. Of those that a mesh axis runs over, the one named last changes fastest.
Arguments:
- amplitudes: float32 [2048, 32768], P(('cd', 'ab')), may hold values from -6 to 6
- integrals: float32 [4096, 32768], P('ab', 'cd'), may hold values from -0.09375 to 0.09375
- orbital_irrep: int32 [1600], replicated, may hold values from 0 to 7
- bra_pairs: int32 [2, 4096], P(None, 'ab'), may hold values from 0 to 1599
- ket_pairs: int32 [2, 32768], P(None, 'cd'), may hold values from 0 to 1599
- slot_pair: int32 [2048], replicated, may hold values from 0 to 2047, each once
Outputs:
- residual: float32 [2048, 4096], P('cd', 'ab')
The draws below stay inside these ranges and needn't reach their ends.
Inputs may be any that keep to these rules, and one draw needn't show every extreme that they name: `slot_pair`: each value appears once; values of 1830 and above mark empty slots.
All inputs are finite; a program needn't handle non-finite values.
Results may differ from the reference program's by a relative error of at most 0.0003.
Values sent between devices are 32-bit elements; how exact they have to be, the bound alone decides.
A program may use at most 64 MiB of HBM per device.

```python
import jax
import jax.numpy as jnp
from jax import lax

V = 1600
AB_DEV = 512
PAIRS = 1830
SLOTS = 2048
AB = 4096
CD = 32768
N_AB = 8


def plant(array, key, smallest, largest):
    place = [jax.random.randint(jax.random.fold_in(key, axis), (), 0, length) for axis, length in enumerate(array.shape)]
    main_axis = array.shape.index(max(array.shape))
    neighbour = place[:main_axis] + [(place[main_axis] + 1) % array.shape[main_axis]] + place[main_axis + 1:]
    return array.at[tuple(place)].set(smallest).at[tuple(neighbour)].set(largest)


def steps_of(stream_key, shape, cuts, smallest, high):
    def one(axis_at, shards_of):
        heights = jax.random.uniform(jax.random.fold_in(jax.random.fold_in(stream_key, 6), axis_at), (shards_of,), jnp.float32, smallest / len(cuts), high / len(cuts))
        return jnp.repeat(jnp.exp(heights), shape[axis_at] // shards_of).reshape((-1,) + (1,) * (len(shape) - axis_at - 1))

    loudness = one(*cuts[0])
    for cut in cuts[1:]:
        loudness = loudness * one(*cut)
    return loudness


def bell_draw(rng, shape, spread, bound, pieces=(), kind=jnp.bfloat16):
    result = jax.random.normal(rng, shape, jnp.float32) * spread
    if len(pieces) > 0:
        result = steps_of(rng, shape, pieces, -0.22, 0.18) * result
    return jnp.clip(result, min=-bound, max=bound).astype(kind)


def setup_inputs(seed: int = 0) -> dict:
    key_list = jax.random.split(jax.random.key(seed), 7)
    return {
        "amplitudes": bell_draw(key_list[0], (SLOTS, CD), 1.0, 6.0, ((0, 512),), jnp.float32),
        "integrals": bell_draw(key_list[1], (AB, CD), (CD // 8) ** -0.5, 0.09375, ((0, 8), (1, 64)), jnp.float32),
        "orbital_irrep": plant(jax.random.randint(key_list[2], (V,), 0, 8), jax.random.fold_in(key_list[2], 1), 0, 7).astype(jnp.int32),
        "bra_pairs": plant(jax.random.randint(key_list[3], (2, AB), 0, V), jax.random.fold_in(key_list[3], 1), 0, V - 1).astype(jnp.int32),
        "ket_pairs": plant(jax.random.randint(key_list[4], (2, CD), 0, V), jax.random.fold_in(key_list[4], 1), 0, V - 1).astype(jnp.int32),
        "slot_pair": jax.random.permutation(key_list[5], SLOTS).astype(jnp.int32),
    }


def reference(amplitudes, integrals, orbital_irrep, bra_pairs, ket_pairs, slot_pair):
    bra_irrep = jnp.bitwise_xor(orbital_irrep[bra_pairs[0]], orbital_irrep[bra_pairs[1]])
    ket_irrep = jnp.bitwise_xor(orbital_irrep[ket_pairs[0]], orbital_irrep[ket_pairs[1]])
    blocks = integrals.reshape(N_AB, AB_DEV, CD)
    block_irrep = bra_irrep.reshape(N_AB, AB_DEV)

    def one_block(item):
        block, irrep_block = item
        selected = jnp.where(irrep_block[:, None] == ket_irrep[None, :], block, jnp.zeros_like(block))
        return jnp.dot(amplitudes, selected.T, precision=lax.Precision.HIGHEST, preferred_element_type=jnp.float32)

    ladder = lax.map(one_block, (blocks, block_irrep))
    ladder = jnp.transpose(ladder, (1, 0, 2)).reshape(SLOTS, AB)
    inverse = jnp.zeros((SLOTS,), jnp.int32).at[slot_pair].set(jnp.arange(SLOTS, dtype=jnp.int32))
    ordered = ladder[inverse]
    keep = jnp.arange(SLOTS, dtype=jnp.int32)[:, None] < PAIRS
    return jnp.where(keep, ordered, jnp.zeros_like(ordered))
```

```python
import jax
import jax.numpy as jnp
from jax import lax
from jax.experimental import pallas as pl
from jax.experimental.pallas import tpu as pltpu
from jax.sharding import PartitionSpec as P

PAIRS = 1830
SLOTS = 2048
NZ, NY, NX, NC = 16, 4, 4, 2
Q = 512
N = 512
SLAB = NZ * NC
CHUNKS = 4
CHUNK = SLAB // CHUNKS
CHUNK_ROWS = CHUNK * 4 * NX * NY
BLOCK = 32
MESH = pl.DeviceIdType.MESH
F32 = jnp.float32
BF16 = jnp.bfloat16


def device(z, y, x, c):
    return {"cd": z * 4 + (y % 2) * 2 + c, "ab": (y // 2) * 4 + x}


def remote(src, dst, send, recv, target):
    return pltpu.make_async_remote_copy(
        src_ref=src, dst_ref=dst, send_sem=send, recv_sem=recv,
        device_id=target, device_id_type=MESH,
    )


def wait_bytes(ref, sem):
    pltpu.make_async_copy(ref, ref, sem).wait()


def offset_of(k):
    odd = k % 2
    return odd * ((k + 1) // 2) + (1 - odd) * ((NZ - k // 2) % NZ)


def kernel(
    amp, ints, bra, ket, place, out,
    every, other, high, low, w_high, w_low, ints_v, part,
    core_out, core_in, y_out, y_keep, y_in, ring_out, ring_a, ring_b,
    sem_ints, s_z, r_own, r_oth, s_y, r_y, s_x, r_x, s_r, r_r,
    s_c, r_c, s_s, r_s, s_a, r_a, s_b, r_b,
):
    cd, ab = lax.axis_index("cd"), lax.axis_index("ab")
    z, c, x = cd // 4, cd % 2, ab % 4
    parity = (cd // 2) % 2
    y = (ab // 4) * 2 + parity

    barrier = pltpu.get_barrier_semaphore()
    greeted = 0
    for k in range(NZ):
        for dc in range(NC):
            if k or dc:
                zz = (z + offset_of(k)) % NZ
                pl.semaphore_signal(barrier, inc=1, device_id=device(zz, y, x, (c + dc) % 2), device_id_type=MESH)
                greeted += 1
    for d in (1, 2, 3):
        pl.semaphore_signal(barrier, inc=1, device_id=device(z, (y + d) % NY, x, c), device_id_type=MESH)
    right, left = device(z, y, (x + 1) % NX, c), device(z, y, (x + 3) % NX, c)
    for target in (right, left):
        pl.semaphore_signal(barrier, inc=1, device_id=target, device_id_type=MESH)
    load = pltpu.make_async_copy(ints, ints_v, sem_ints)
    load.start()
    pl.semaphore_wait(barrier, greeted + 5)

    def slab(zz, half, core):
        return amp.at[:, pl.ds(pl.multiple_of(zz * 2048 + half * 1024 + core * 512, 512), Q)]

    def send_z(k, dc):
        zz, cc = (z + offset_of(k)) % NZ, (c + dc) % 2
        entry, g, target = k * 2 + c, k // (NZ // CHUNKS), device(zz, y, x, cc)
        remote(slab(zz, 1 - parity, cc), other.at[entry], s_z, r_oth.at[g], target).start()
        remote(slab(zz, parity, cc), every.at[x, y, entry], s_z, r_own.at[g], target).start()

    pltpu.make_async_copy(slab(z, 1 - parity, c), other.at[c], r_oth.at[0]).start()
    pltpu.make_async_copy(slab(z, parity, c), every.at[x, y, c], r_own.at[0]).start()
    send_z(0, 1)

    @pl.loop(1, NZ)
    def _(k):
        send_z(k, 0)
        send_z(k, 1)

    load.wait()
    for i in range(4):
        rows = pl.ds(i * 128, 128)
        picked = jnp.where(bra[rows, :] == ket[...], ints_v[rows, :], 0.0)
        turned = picked.T
        top = turned.astype(BF16)
        w_high[:, rows] = top
        w_low[:, rows] = (turned - top.astype(F32)).astype(BF16)

    def span(g):
        return pl.ds(g * CHUNK, CHUNK)

    def step_y(g):
        wait_bytes(every.at[x, y, span(g)], r_own.at[g])
        own = every.at[x, y, span(g)]
        remote(own, own, s_y.at[0], r_y.at[g, 2], device(z, (y + 2) % NY, x, c)).start()
        remote(own, own, s_x, r_x.at[g, 0, 0], right).start()
        remote(own, own, s_x, r_x.at[g, 1, 0], left).start()
        wait_bytes(other.at[span(g)], r_oth.at[g])
        for d in (1, 3):
            remote(
                other.at[span(g)], every.at[x, y, span(g)], s_y.at[0], r_y.at[g, d],
                device(z, (y + d) % NY, x, c),
            ).start()

    def step_x(g):
        for d in (1, 3, 2):
            ref = every.at[x, (y + NY - d) % NY, span(g)]
            wait_bytes(ref, r_y.at[g, d])
            remote(ref, ref, s_x, r_x.at[g, 0, d], right).start()
            remote(ref, ref, s_x, r_x.at[g, 1, d], left).start()

    def step_relay(g):
        for d in (0, 1, 3, 2):
            yy = (y + NY - d) % NY
            from_left, from_right = every.at[(x + 3) % NX, yy, span(g)], every.at[(x + 1) % NX, yy, span(g)]
            if d in (0, 1):
                wait_bytes(from_left, r_x.at[g, 0, d])
                remote(from_left, from_left, s_r, r_r.at[g, d], right).start()
            else:
                wait_bytes(from_right, r_x.at[g, 1, d])
                remote(from_right, from_right, s_r, r_r.at[g, d], left).start()

    def step_dot(g):
        for d in (0, 1, 3, 2):
            yy = (y + NY - d) % NY
            from_left, from_right = every.at[(x + 3) % NX, yy, span(g)], every.at[(x + 1) % NX, yy, span(g)]
            if d in (0, 1):
                wait_bytes(from_right, r_x.at[g, 1, d])
            else:
                wait_bytes(from_left, r_x.at[g, 0, d])
            wait_bytes(every.at[(x + 2) % NX, yy, span(g)], r_r.at[g, d])

        for xx in range(NX):
            for yy in range(NY):
                value = every[xx, yy, g * CHUNK:(g + 1) * CHUNK].reshape(CHUNK * 4, Q)
                top = value.astype(BF16)
                rows = pl.ds((xx * NY + yy) * CHUNK * 4, CHUNK * 4)
                high[rows, :] = top
                low[rows, :] = (value - top.astype(F32)).astype(BF16)
        for i in range(0, CHUNK_ROWS, 256):
            rows = pl.ds(i, 256)
            result = jnp.dot(high[rows, :], w_high[...], preferred_element_type=F32)
            result += jnp.dot(high[rows, :], w_low[...], preferred_element_type=F32)
            result += jnp.dot(low[rows, :], w_high[...], preferred_element_type=F32)
            part[pl.ds(g * CHUNK_ROWS + i, 256)] = result.reshape(256, 4, 128)

    for t in range(CHUNKS + 3):
        if t < CHUNKS:
            step_y(t)
        if 1 <= t < CHUNKS + 1:
            step_x(t - 1)
        if 2 <= t < CHUNKS + 2:
            step_relay(t - 2)
        if t >= 3:
            step_dot(t - 3)

    def target_z(t):
        return (z + (8 - t // 2 if t % 2 == 0 else 9 + t // 2) % NZ) % NZ if t < 15 else z

    def gather(t, half, core, use):
        base = target_z(t) * 128 + half * 64 + core * 32

        @pl.loop(0, BLOCK, unroll=8)
        def _(i):
            use(i, part[place[base + i]])

    partner_core = device(z, y, x, 1 - c)
    partner_y = device(z, y + 1 - 2 * parity, x, c)
    up, down = device((z + 1) % NZ, y, x, c), device((z + NZ - 1) % NZ, y, x, c)

    def step_gather(t):
        for half in range(2):
            def put(i, row):
                core_out[t, half, i] = row
            gather(t, half, 1 - c, put)
        remote(core_out.at[t], core_in.at[t], s_c, r_c.at[t], partner_core).start()

    def step_core(t):
        wait_bytes(core_in.at[t], r_c.at[t])

        def put_out(i, row):
            y_out[t, i] = row + core_in[t, 1 - parity, i]
        gather(t, 1 - parity, c, put_out)
        remote(y_out.at[t], y_in.at[t], s_s, r_s.at[t], partner_y).start()

        def put_keep(i, row):
            y_keep[t, i] = row + core_in[t, parity, i]
        gather(t, parity, c, put_keep)

    def step_ring(t):
        s = t // 2
        wait_bytes(y_in.at[t], r_s.at[t])
        value = y_keep[t] + y_in[t]
        if t == 15:
            wait_bytes(ring_a.at[7], r_a.at[7])
            wait_bytes(ring_b.at[6], r_b.at[6])
            value = value + ring_a[7] + ring_b[6]
            row = lax.broadcasted_iota(jnp.int32, (BLOCK, 4, 128), 0) + cd * BLOCK
            out[...] = jnp.where(row < PAIRS, value, 0.0)
        elif t % 2 == 0:
            if s:
                wait_bytes(ring_a.at[s - 1], r_a.at[s - 1])
                value = value + ring_a[s - 1]
            ring_out[t] = value
            remote(ring_out.at[t], ring_a.at[s], s_a, r_a.at[s], up).start()
        else:
            if s:
                wait_bytes(ring_b.at[s - 1], r_b.at[s - 1])
                value = value + ring_b[s - 1]
            ring_out[t] = value
            remote(ring_out.at[t], ring_b.at[s], s_b, r_b.at[s], down).start()

    for t in range(16 + 4):
        if t < 16:
            step_gather(t)
        if 1 <= t < 17:
            step_core(t - 1)
        if t >= 4:
            step_ring(t - 4)

    wait_bytes(every.at[0, 0, pl.ds(0, 31)], s_z)
    wait_bytes(every.at[0, 0, pl.ds(0, 31)], s_z)
    for d in range(3):
        wait_bytes(every.at[0, d], s_y.at[0])
    wait_bytes(every.at[0], s_x)
    wait_bytes(every.at[0], s_x)
    wait_bytes(every.at[0], s_r)
    wait_bytes(core_in, s_c)
    wait_bytes(y_in, s_s)
    wait_bytes(ring_a, s_a)
    wait_bytes(ring_b, s_b)


def on_device(amplitudes, integrals, orbital_irrep, bra_pairs, ket_pairs, slot_pair):
    bra = jnp.bitwise_xor(orbital_irrep[bra_pairs[0]], orbital_irrep[bra_pairs[1]])
    ket = jnp.bitwise_xor(orbital_irrep[ket_pairs[0]], orbital_irrep[ket_pairs[1]])
    slot = jnp.arange(SLOTS, dtype=jnp.int32)
    src_ab, src_cd = slot // 4 % 8, slot // 32
    src_x, src_y = src_ab % 4, src_ab // 4 * 2 + src_cd // 2 % 2
    dz = (lax.axis_index("cd") // 4 - src_cd // 4) % NZ
    k = jnp.where(dz == 0, 0, jnp.where(dz <= 8, 2 * dz - 1, 2 * (NZ - dz)))
    entry = k * 2 + src_cd % 2
    spot = (
        entry // CHUNK * CHUNK_ROWS
        + ((src_x * NY + src_y) * CHUNK + entry % CHUNK) * 4
        + slot % 4
    )
    place = jnp.sum(
        jnp.where(slot_pair[None, :] == slot[:, None], spot[None, :], 0), axis=1
    ).astype(jnp.int32)

    dma = pltpu.SemaphoreType.DMA
    result = pl.pallas_call(
        kernel,
        out_shape=jax.ShapeDtypeStruct((BLOCK, 4, 128), F32),
        in_specs=[
            pl.BlockSpec(memory_space=pl.ANY),
            pl.BlockSpec(memory_space=pl.ANY),
            pl.BlockSpec(memory_space=pltpu.VMEM),
            pl.BlockSpec(memory_space=pltpu.VMEM),
            pl.BlockSpec(memory_space=pltpu.SMEM),
        ],
        out_specs=pl.BlockSpec(memory_space=pltpu.VMEM),
        scratch_shapes=[
            pltpu.VMEM((NX, NY, SLAB, 4, Q), F32),
            pltpu.VMEM((SLAB, 4, Q), F32),
            pltpu.VMEM((CHUNK_ROWS, Q), BF16),
            pltpu.VMEM((CHUNK_ROWS, Q), BF16),
            pltpu.VMEM((Q, N), BF16),
            pltpu.VMEM((Q, N), BF16),
            pltpu.VMEM((N, Q), F32),
            pltpu.VMEM((SLOTS, 4, 128), F32),
            pltpu.VMEM((16, 2, BLOCK, 4, 128), F32),
            pltpu.VMEM((16, 2, BLOCK, 4, 128), F32),
            pltpu.VMEM((16, BLOCK, 4, 128), F32),
            pltpu.VMEM((16, BLOCK, 4, 128), F32),
            pltpu.VMEM((16, BLOCK, 4, 128), F32),
            pltpu.VMEM((15, BLOCK, 4, 128), F32),
            pltpu.VMEM((8, BLOCK, 4, 128), F32),
            pltpu.VMEM((7, BLOCK, 4, 128), F32),
            dma,
            dma, dma((CHUNKS,)), dma((CHUNKS,)),
            dma((1,)), dma((CHUNKS, 4)),
            dma, dma((CHUNKS, 2, 4)),
            dma, dma((CHUNKS, 4)),
            dma, dma((16,)),
            dma, dma((16,)),
            dma, dma((8,)),
            dma, dma((7,)),
        ],
        compiler_params=pltpu.CompilerParams(
            collective_id=0, has_side_effects=True, vmem_limit_bytes=48 << 20
        ),
        name="ladder",
    )(amplitudes, integrals, bra[:, None], ket[None, :], place)
    return result.reshape(BLOCK, N)


def solution(mesh):
    in_specs = (P(("cd", "ab"), None), P("ab", "cd"), P(), P(None, "ab"), P(None, "cd"), P())
    out_specs = P("cd", "ab")
    return jax.shard_map(
        on_device, mesh=mesh, in_specs=in_specs, out_specs=out_specs, check_vma=False
    )
```

```python
import jax
import jax.numpy as jnp
from jax import lax
from jax.experimental import pallas as pl
from jax.experimental.pallas import tpu as pltpu
from jax.sharding import PartitionSpec as P

PAIRS = 1830
SLOTS = 2048
NZ, NY, NX, NC = 16, 4, 4, 2
Q = 512
N = 512
SLAB = NZ * NC
CHUNKS = 8
STEPS = NZ // CHUNKS
CHUNK = SLAB // CHUNKS
CHUNK_ROWS = CHUNK * 4 * NX * NY
TABLE = 13
BLOCK = 32
ORDER = (
    ("select", 0), ("own", 0), ("oth", 0), ("own", 1), ("oth", 1), ("ownL", 0), ("ownR", 0), ("othL", 0),
    ("othR", 0), ("yown", 0), ("ownL", 1), ("ownR", 1), ("own", 2), ("oth", 2), ("othL", 1), ("othR", 1),
    ("yown", 1), ("oth2", 0), ("d2L", 0), ("place", 0), ("d2R", 0), ("own", 3), ("oth", 3), ("ownR", 2),
    ("ownL", 2), ("othR", 2), ("yown", 2), ("othL", 2), ("d2R", 1), ("oth2", 1), ("d2L", 1), ("own", 4),
    ("oth", 4), ("ownL", 3), ("ownR", 3), ("othL", 3), ("yown", 3), ("othR", 3), ("oth2", 2), ("d2L", 2),
    ("dot", 0), ("d2R", 2), ("ownL", 4), ("own", 5), ("oth", 5), ("othL", 4), ("ownR", 4), ("yown", 4),
    ("othR", 4), ("oth2", 3), ("d2R", 3), ("d2L", 3), ("dot", 1), ("own", 6), ("oth", 6), ("ownR", 5),
    ("ownL", 5), ("othR", 5), ("othL", 5), ("yown", 5), ("d2R", 4), ("d2L", 4), ("own", 7), ("oth", 7),
    ("oth2", 4), ("ownL", 6), ("othL", 6), ("ownR", 6), ("dot", 2), ("othR", 6), ("oth2", 5), ("yown", 6),
    ("d2R", 5), ("d2L", 5), ("dot", 3), ("ownL", 7), ("ownR", 7), ("othL", 7), ("othR", 7), ("yown", 7),
    ("oth2", 6), ("d2L", 6), ("d2R", 6), ("dot", 4), ("oth2", 7), ("d2R", 7), ("dot", 5), ("d2L", 7),
    ("dot", 6), ("dot", 7),
)
MESH = pl.DeviceIdType.MESH
F32 = jnp.float32
BF16 = jnp.bfloat16


def device(z, y, x, c):
    return {"cd": z * 4 + (y % 2) * 2 + c, "ab": (y // 2) * 4 + x}


def remote(src, dst, send, recv, target):
    return pltpu.make_async_remote_copy(
        src_ref=src, dst_ref=dst, send_sem=send, recv_sem=recv,
        device_id=target, device_id_type=MESH,
    )


def wait_bytes(ref, sem):
    pltpu.make_async_copy(ref, ref, sem).wait()


def offset_of(k):
    odd = k % 2
    return odd * ((k + 1) // 2) + (1 - odd) * ((NZ - k // 2) % NZ)


def kernel(
    amp, ints, table, bra, ket, slots, out,
    every, other, high, low, w_high, w_low, ints_v, part, place_v, place,
    core_out, core_in, y_out, y_keep, y_in, ring_out, ring_a, ring_b,
    sem_ints, sem_place, s_z, r_own, r_oth, s_w, s_y, r_y, s_x, r_x, r_ox, s_r, r_r, r_ro,
    s_c, r_c, s_s, r_s, s_a, r_a, s_b, r_b,
):
    cd, ab = lax.axis_index("cd"), lax.axis_index("ab")
    z, c, x = cd // 4, cd % 2, ab % 4
    parity = (cd // 2) % 2
    y = (ab // 4) * 2 + parity

    barrier = pltpu.get_barrier_semaphore()
    greeted = 0
    for k in range(NZ):
        for dc in range(NC):
            if k or dc:
                zz = (z + offset_of(k)) % NZ
                pl.semaphore_signal(barrier, inc=1, device_id=device(zz, y, x, (c + dc) % 2), device_id_type=MESH)
                greeted += 1
    for d in (1, 2, 3):
        pl.semaphore_signal(barrier, inc=1, device_id=device(z, (y + d) % NY, x, c), device_id_type=MESH)
    right, left = device(z, y, (x + 1) % NX, c), device(z, y, (x + 3) % NX, c)
    for target in (right, left):
        pl.semaphore_signal(barrier, inc=1, device_id=target, device_id_type=MESH)
    load = pltpu.make_async_copy(ints, ints_v, sem_ints)
    load.start()
    pl.semaphore_wait(barrier, greeted + 5)

    def slab(zz, half, core):
        return amp.at[:, pl.ds(pl.multiple_of(zz * 2048 + half * 1024 + core * 512, 512), Q)]

    def send_z(k, dc):
        zz, cc = (z + offset_of(k)) % NZ, (c + dc) % 2
        entry, g, target = k * 2 + c, k // STEPS, device(zz, y, x, cc)
        remote(slab(zz, 1 - parity, cc), other.at[x, entry], s_z, r_oth.at[g], target).start()
        remote(slab(zz, parity, cc), every.at[x, y, entry], s_z, r_own.at[g], target).start()

    pltpu.make_async_copy(slab(z, 1 - parity, c), other.at[x, c], r_oth.at[0]).start()
    pltpu.make_async_copy(slab(z, parity, c), every.at[x, y, c], r_own.at[0]).start()
    send_z(0, 1)

    @pl.loop(1, NZ)
    def _(k):
        send_z(k, 0)
        send_z(k, 1)

    def irreps(pairs):
        index = jnp.concatenate([pairs[:, i * 128:(i + 1) * 128] for i in range(4)], axis=0)
        found = jnp.zeros((8, 128), jnp.int32)
        for i in range(TABLE):
            row = jnp.broadcast_to(table[i:i + 1, :], (8, 128))
            value = jnp.take_along_axis(row, index & 127, axis=1, mode="promise_in_bounds")
            found = jnp.where(index >> 7 == i, value, found)
        return [
            (found[2 * i:2 * i + 1] ^ found[2 * i + 1:2 * i + 2]).astype(F32) for i in range(4)
        ]

    def column(row):
        return jnp.broadcast_to(row, (128, 128)).T

    def select_integrals():
        bras, kets = irreps(bra), irreps(ket)
        load.wait()
        for i in range(4):
            bra_irrep = column(bras[i])
            for j in range(4):
                p, q = pl.ds(i * 128, 128), pl.ds(j * 128, 128)
                turned = jnp.where(bra_irrep == kets[j], ints_v[p, q], 0.0).T
                top = turned.astype(BF16)
                w_high[q, p] = top
                w_low[q, p] = (turned - top.astype(F32)).astype(BF16)

    def place_rows():
        place_v[...] = jnp.zeros((16, 128), jnp.int32)
        u = lax.broadcasted_iota(jnp.int32, (128, 128), 0)
        lane = lax.broadcasted_iota(jnp.int32, (128, 128), 1)
        src_x, src_y, src_c = (u >> 2) & 3, ((u >> 4) & 1) * 2 + (u >> 6), (u >> 5) & 1
        fixed = ((src_x * NY + src_y) * CHUNK + src_c) * 4 + (u & 3)

        @pl.loop(0, NZ)
        def _(j):
            dz = (z + NZ - j) % NZ
            k = jnp.where(dz == 0, 0, jnp.where(dz <= 8, 2 * dz - 1, 2 * (NZ - dz)))
            spot = fixed + (k // STEPS * CHUNK_ROWS + k % STEPS * 8)
            pair = column(slots[pl.ds(j, 1), :].astype(F32)).astype(jnp.int32)
            for i in range(16):
                hit = jnp.where(pair == lane + i * 128, spot, 0)
                place_v[i:i + 1, :] += jnp.sum(hit, axis=0, keepdims=True)

        copy = pltpu.make_async_copy(place_v, place, sem_place)
        copy.start()
        copy.wait()

    def span(g):
        return pl.ds(g * CHUNK, CHUNK)

    def row_y(d):
        return (y + NY - d) % NY

    def row_x(d):
        return (x + d) % NX

    def send_x(ref, sems):
        remote(ref, ref, s_x, sems[0], right).start()
        remote(ref, ref, s_x, sems[1], left).start()

    def relay(ref, sem, target):
        remote(ref, ref, s_r, sem, target).start()

    def send_y(g, col):
        for d in (1, 3):
            remote(
                other.at[row_x(col), span(g)], every.at[row_x(col), y, span(g)], s_y,
                r_y.at[g, col, d], device(z, (y + d) % NY, x, c),
            ).start()

    def step_own(g):
        ref = every.at[x, y, span(g)]
        wait_bytes(ref, r_own.at[g])
        remote(ref, ref, s_w, r_y.at[g, 0, 2], device(z, (y + 2) % NY, x, c)).start()
        send_x(ref, (r_x.at[g, 0, 0], r_x.at[g, 1, 0]))

    def step_oth(g):
        ref = other.at[x, span(g)]
        wait_bytes(ref, r_oth.at[g])
        send_x(ref, (r_ox.at[g, 0], r_ox.at[g, 1]))
        send_y(g, 0)

    def step_yown(g):
        ref = every.at[x, row_y(2), span(g)]
        wait_bytes(ref, r_y.at[g, 0, 2])
        send_x(ref, (r_x.at[g, 0, 2], r_x.at[g, 1, 2]))

    def step_ownl(g):
        ref = every.at[row_x(3), y, span(g)]
        wait_bytes(ref, r_x.at[g, 0, 0])
        relay(ref, r_r.at[g, 0], right)

    def step_ownr(g):
        wait_bytes(every.at[row_x(1), y, span(g)], r_x.at[g, 1, 0])

    def step_d2l(g):
        wait_bytes(every.at[row_x(3), row_y(2), span(g)], r_x.at[g, 0, 2])

    def step_d2r(g):
        ref = every.at[row_x(1), row_y(2), span(g)]
        wait_bytes(ref, r_x.at[g, 1, 2])
        relay(ref, r_r.at[g, 2], left)

    def step_othl(g):
        ref = other.at[row_x(3), span(g)]
        wait_bytes(ref, r_ox.at[g, 0])
        if g % 2:
            relay(ref, r_ro.at[g], right)
        send_y(g, 3)

    def step_othr(g):
        ref = other.at[row_x(1), span(g)]
        wait_bytes(ref, r_ox.at[g, 1])
        if g % 2 == 0:
            relay(ref, r_ro.at[g], left)
        send_y(g, 1)

    def step_oth2(g):
        wait_bytes(other.at[row_x(2), span(g)], r_ro.at[g])
        send_y(g, 2)

    def step_dot(g):
        for d in (0, 2):
            wait_bytes(every.at[row_x(2), row_y(d), span(g)], r_r.at[g, d])
        for col in (0, 1, 3, 2):
            for d in (1, 3):
                wait_bytes(every.at[row_x(col), row_y(d), span(g)], r_y.at[g, col, d])

        for xx in range(NX):
            for yy in range(NY):
                value = every[xx, yy, g * CHUNK:(g + 1) * CHUNK].reshape(CHUNK * 4, Q)
                top = value.astype(BF16)
                rows = pl.ds((xx * NY + yy) * CHUNK * 4, CHUNK * 4)
                high[rows, :] = top
                low[rows, :] = (value - top.astype(F32)).astype(BF16)
        result = jnp.dot(high[...], w_high[...], preferred_element_type=F32)
        result += jnp.dot(high[...], w_low[...], preferred_element_type=F32)
        result += jnp.dot(low[...], w_high[...], preferred_element_type=F32)
        part[pl.ds(g * CHUNK_ROWS, CHUNK_ROWS)] = result.reshape(CHUNK_ROWS, 4, 128)

    steps = {
        "own": step_own, "oth": step_oth, "yown": step_yown, "ownL": step_ownl, "ownR": step_ownr,
        "d2L": step_d2l, "d2R": step_d2r, "othL": step_othl, "othR": step_othr, "oth2": step_oth2,
        "dot": step_dot,
    }
    for name, g in ORDER:
        if name == "select":
            select_integrals()
        elif name == "place":
            place_rows()
        else:
            steps[name](g)

    def target_z(t):
        return (z + (8 - t // 2 if t % 2 == 0 else 9 + t // 2) % NZ) % NZ if t < 15 else z

    def gather(t, half, core, use):
        base = target_z(t) * 128 + half * 64 + core * 32

        @pl.loop(0, BLOCK, unroll=8)
        def _(i):
            use(i, part[place[base // 128, base % 128 + i]])

    partner_core = device(z, y, x, 1 - c)
    partner_y = device(z, y + 1 - 2 * parity, x, c)
    up, down = device((z + 1) % NZ, y, x, c), device((z + NZ - 1) % NZ, y, x, c)

    def step_gather(t):
        for half in range(2):
            def put(i, row):
                core_out[t, half, i] = row
            gather(t, half, 1 - c, put)
        remote(core_out.at[t], core_in.at[t], s_c, r_c.at[t], partner_core).start()

    def step_core(t):
        wait_bytes(core_in.at[t], r_c.at[t])

        def put_out(i, row):
            y_out[t, i] = row + core_in[t, 1 - parity, i]
        gather(t, 1 - parity, c, put_out)
        remote(y_out.at[t], y_in.at[t], s_s, r_s.at[t], partner_y).start()

        def put_keep(i, row):
            y_keep[t, i] = row + core_in[t, parity, i]
        gather(t, parity, c, put_keep)

    def step_ring(t):
        s = t // 2
        wait_bytes(y_in.at[t], r_s.at[t])
        value = y_keep[t] + y_in[t]
        if t == 15:
            wait_bytes(ring_a.at[7], r_a.at[7])
            wait_bytes(ring_b.at[6], r_b.at[6])
            value = value + ring_a[7] + ring_b[6]
            row = lax.broadcasted_iota(jnp.int32, (BLOCK, 4, 128), 0) + cd * BLOCK
            out[...] = jnp.where(row < PAIRS, value, 0.0)
        elif t % 2 == 0:
            if s:
                wait_bytes(ring_a.at[s - 1], r_a.at[s - 1])
                value = value + ring_a[s - 1]
            ring_out[t] = value
            remote(ring_out.at[t], ring_a.at[s], s_a, r_a.at[s], up).start()
        else:
            if s:
                wait_bytes(ring_b.at[s - 1], r_b.at[s - 1])
                value = value + ring_b[s - 1]
            ring_out[t] = value
            remote(ring_out.at[t], ring_b.at[s], s_b, r_b.at[s], down).start()

    for t in range(16 + 4):
        if t < 16:
            step_gather(t)
        if 1 <= t < 17:
            step_core(t - 1)
        if t >= 4:
            step_ring(t - 4)

    wait_bytes(every.at[0, 0, pl.ds(0, 31)], s_z)
    wait_bytes(every.at[0, 0, pl.ds(0, 31)], s_z)
    for sem, units in ((s_w, 1), (s_y, 8), (s_x, 6), (s_r, 3)):
        for _ in range(units):
            wait_bytes(every.at[0, 0], sem)
    wait_bytes(core_in, s_c)
    wait_bytes(y_in, s_s)
    wait_bytes(ring_a, s_a)
    wait_bytes(ring_b, s_b)


def on_device(amplitudes, integrals, orbital_irrep, bra_pairs, ket_pairs, slot_pair):
    table = jnp.pad(orbital_irrep, (0, 16 * 128 - orbital_irrep.shape[0])).reshape(16, 128)
    dma = pltpu.SemaphoreType.DMA
    result = pl.pallas_call(
        kernel,
        out_shape=jax.ShapeDtypeStruct((BLOCK, 4, 128), F32),
        in_specs=[
            pl.BlockSpec(memory_space=pl.ANY),
            pl.BlockSpec(memory_space=pl.ANY),
            pl.BlockSpec(memory_space=pltpu.VMEM),
            pl.BlockSpec(memory_space=pltpu.VMEM),
            pl.BlockSpec(memory_space=pltpu.VMEM),
            pl.BlockSpec(memory_space=pltpu.VMEM),
        ],
        out_specs=pl.BlockSpec(memory_space=pltpu.VMEM),
        scratch_shapes=[
            pltpu.VMEM((NX, NY, SLAB, 4, Q), F32),
            pltpu.VMEM((NX, SLAB, 4, Q), F32),
            pltpu.VMEM((CHUNK_ROWS, Q), BF16),
            pltpu.VMEM((CHUNK_ROWS, Q), BF16),
            pltpu.VMEM((Q, N), BF16),
            pltpu.VMEM((Q, N), BF16),
            pltpu.VMEM((N, Q), F32),
            pltpu.VMEM((SLOTS, 4, 128), F32),
            pltpu.VMEM((16, 128), jnp.int32),
            pltpu.SMEM((16, 128), jnp.int32),
            pltpu.VMEM((16, 2, BLOCK, 4, 128), F32),
            pltpu.VMEM((16, 2, BLOCK, 4, 128), F32),
            pltpu.VMEM((16, BLOCK, 4, 128), F32),
            pltpu.VMEM((16, BLOCK, 4, 128), F32),
            pltpu.VMEM((16, BLOCK, 4, 128), F32),
            pltpu.VMEM((15, BLOCK, 4, 128), F32),
            pltpu.VMEM((8, BLOCK, 4, 128), F32),
            pltpu.VMEM((7, BLOCK, 4, 128), F32),
            dma, dma,
            dma, dma((CHUNKS,)), dma((CHUNKS,)),
            dma, dma, dma((CHUNKS, 4, 4)),
            dma, dma((CHUNKS, 2, 4)), dma((CHUNKS, 2)),
            dma, dma((CHUNKS, 4)), dma((CHUNKS,)),
            dma, dma((16,)),
            dma, dma((16,)),
            dma, dma((8,)),
            dma, dma((7,)),
        ],
        compiler_params=pltpu.CompilerParams(
            collective_id=0, has_side_effects=True, vmem_limit_bytes=48 << 20
        ),
        name="ladder",
    )(amplitudes, integrals, table, bra_pairs, ket_pairs, slot_pair.reshape(16, 128))
    return result.reshape(BLOCK, N)


def solution(mesh):
    in_specs = (P(("cd", "ab"), None), P("ab", "cd"), P(), P(None, "ab"), P(None, "cd"), P())
    out_specs = P("cd", "ab")
    return jax.shard_map(
        on_device, mesh=mesh, in_specs=in_specs, out_specs=out_specs, check_vma=False
    )
```

```python
import jax
import jax.numpy as jnp
from jax import lax
from jax.experimental import pallas as pl
from jax.experimental.pallas import tpu as pltpu
from jax.sharding import PartitionSpec as P

PAIRS = 1830
SLOTS = 2048
NZ, NY, NX, NC = 16, 4, 4, 2
Q = 512
N = 512
SLAB = NZ * NC
CHUNKS = 8
STEPS = NZ // CHUNKS
CHUNK = SLAB // CHUNKS
CHUNK_ROWS = CHUNK * 4 * NX * NY
TABLE = 13
BLOCK = 32
ORDER = (
    ("select", 0), ("own", 0), ("oth", 0), ("own", 1), ("oth", 1), ("ownL", 0), ("ownR", 0), ("othL", 0),
    ("othR", 0), ("yown", 0), ("ownL", 1), ("ownR", 1), ("own", 2), ("oth", 2), ("othL", 1), ("othR", 1),
    ("yown", 1), ("oth2", 0), ("d2L", 0), ("place", 0), ("d2R", 0), ("own", 3), ("oth", 3), ("ownR", 2),
    ("ownL", 2), ("othR", 2), ("yown", 2), ("othL", 2), ("d2R", 1), ("oth2", 1), ("d2L", 1), ("own", 4),
    ("oth", 4), ("ownL", 3), ("ownR", 3), ("othL", 3), ("yown", 3), ("othR", 3), ("oth2", 2), ("d2L", 2),
    ("dot", 0), ("d2R", 2), ("ownL", 4), ("own", 5), ("oth", 5), ("othL", 4), ("ownR", 4), ("yown", 4),
    ("othR", 4), ("oth2", 3), ("d2R", 3), ("d2L", 3), ("dot", 1), ("own", 6), ("oth", 6), ("ownR", 5),
    ("ownL", 5), ("othR", 5), ("othL", 5), ("yown", 5), ("d2R", 4), ("d2L", 4), ("own", 7), ("oth", 7),
    ("oth2", 4), ("ownL", 6), ("othL", 6), ("ownR", 6), ("dot", 2), ("othR", 6), ("oth2", 5), ("yown", 6),
    ("d2R", 5), ("d2L", 5), ("dot", 3), ("ownL", 7), ("ownR", 7), ("othL", 7), ("othR", 7), ("yown", 7),
    ("oth2", 6), ("d2L", 6), ("d2R", 6), ("dot", 4), ("oth2", 7), ("d2R", 7), ("dot", 5), ("d2L", 7),
    ("dot", 6), ("dot", 7),
)
WIDE = 8
NARROW = BLOCK - WIDE
PIECES = 2
PIECE = NARROW // PIECES
SUMS = (
    ("gather", 0, 0), ("gather", 1, 0), ("gather", 2, 0), ("gather", 3, 0), ("gather", 4, 0),
    ("gather", 5, 0), ("gather", 6, 0), ("gather", 7, 0), ("core", 0, 0), ("wide", 0, 0), ("core", 1, 0),
    ("core", 2, 0), ("wide", 2, 0), ("core", 3, 0), ("wide", 3, 0), ("core", 4, 0), ("wide", 4, 0),
    ("core", 5, 0), ("core", 6, 0), ("core", 7, 0), ("wide", 7, 0), ("sum", 0, 0), ("wide", 1, 0),
    ("sum", 0, 1), ("gather", 8, 0), ("gather", 9, 0), ("sum", 2, 0), ("gather", 10, 0), ("sum", 2, 1),
    ("wide", 6, 0), ("sum", 3, 0), ("gather", 11, 0), ("sum", 3, 1), ("gather", 12, 0), ("sum", 4, 0),
    ("gather", 13, 0), ("core", 8, 0), ("wide", 8, 0), ("sum", 4, 1), ("core", 9, 0), ("sum", 1, 0),
    ("core", 10, 0), ("core", 11, 0), ("wide", 11, 0), ("core", 12, 0), ("wide", 12, 0), ("sum", 1, 1),
    ("wide", 5, 0), ("core", 13, 0), ("sum", 7, 0), ("sum", 7, 1), ("sum", 8, 0), ("sum", 6, 0),
    ("sum", 8, 1), ("gather", 14, 0), ("wide", 10, 0), ("gather", 15, 0), ("sum", 5, 0), ("sum", 6, 1),
    ("sum", 11, 0), ("sum", 5, 1), ("core", 14, 0), ("sum", 11, 1), ("core", 15, 0), ("sum", 12, 0),
    ("sum", 12, 1), ("wide", 9, 0), ("sum", 10, 0), ("wide", 14, 0), ("sum", 9, 0), ("sum", 10, 1),
    ("sum", 9, 1), ("sum", 14, 0), ("wide", 13, 0), ("sum", 13, 0), ("sum", 14, 1), ("sum", 13, 1),
    ("wide", 15, 0), ("sum", 15, 0), ("sum", 15, 1),
)
MESH = pl.DeviceIdType.MESH
F32 = jnp.float32
BF16 = jnp.bfloat16


def device(z, y, x, c):
    return {"cd": z * 4 + (y % 2) * 2 + c, "ab": (y // 2) * 4 + x}


def remote(src, dst, send, recv, target):
    return pltpu.make_async_remote_copy(
        src_ref=src, dst_ref=dst, send_sem=send, recv_sem=recv,
        device_id=target, device_id_type=MESH,
    )


def wait_bytes(ref, sem):
    pltpu.make_async_copy(ref, ref, sem).wait()


def offset_of(k):
    odd = k % 2
    return odd * ((k + 1) // 2) + (1 - odd) * ((NZ - k // 2) % NZ)


def kernel(
    amp, ints, table, bra, ket, slots, out,
    every, other, high, low, w_high, w_low, ints_v, part, place_v, place,
    core_out, core_in, y_out, y_keep, y_in, y_last, wide, sum_out, sum_in, wide_out, wide_in,
    sem_ints, sem_place, s_z, r_own, r_oth, s_w, s_y, r_y, s_x, r_x, r_ox, s_r, r_r, r_ro,
    s_c, r_c, s_s, r_s, s_sum, r_sum, s_wide, r_wide, s_last, r_last,
):
    cd, ab = lax.axis_index("cd"), lax.axis_index("ab")
    z, c, x = cd // 4, cd % 2, ab % 4
    parity = (cd // 2) % 2
    y = (ab // 4) * 2 + parity

    barrier = pltpu.get_barrier_semaphore()
    greeted = 0
    for k in range(NZ):
        for dc in range(NC):
            if k or dc:
                zz = (z + offset_of(k)) % NZ
                pl.semaphore_signal(barrier, inc=1, device_id=device(zz, y, x, (c + dc) % 2), device_id_type=MESH)
                greeted += 1
    for d in (1, 2, 3):
        pl.semaphore_signal(barrier, inc=1, device_id=device(z, (y + d) % NY, x, c), device_id_type=MESH)
    right, left = device(z, y, (x + 1) % NX, c), device(z, y, (x + 3) % NX, c)
    for target in (right, left):
        pl.semaphore_signal(barrier, inc=1, device_id=target, device_id_type=MESH)
    load = pltpu.make_async_copy(ints, ints_v, sem_ints)
    load.start()
    pl.semaphore_wait(barrier, greeted + 5)

    def slab(zz, half, core):
        return amp.at[:, pl.ds(pl.multiple_of(zz * 2048 + half * 1024 + core * 512, 512), Q)]

    def send_z(k, dc):
        zz, cc = (z + offset_of(k)) % NZ, (c + dc) % 2
        entry, g, target = k * 2 + c, k // STEPS, device(zz, y, x, cc)
        remote(slab(zz, 1 - parity, cc), other.at[x, entry], s_z, r_oth.at[g], target).start()
        remote(slab(zz, parity, cc), every.at[x, y, entry], s_z, r_own.at[g], target).start()

    pltpu.make_async_copy(slab(z, 1 - parity, c), other.at[x, c], r_oth.at[0]).start()
    pltpu.make_async_copy(slab(z, parity, c), every.at[x, y, c], r_own.at[0]).start()
    send_z(0, 1)

    @pl.loop(1, NZ)
    def _(k):
        send_z(k, 0)
        send_z(k, 1)

    def irreps(pairs):
        index = jnp.concatenate([pairs[:, i * 128:(i + 1) * 128] for i in range(4)], axis=0)
        found = jnp.zeros((8, 128), jnp.int32)
        for i in range(TABLE):
            row = jnp.broadcast_to(table[i:i + 1, :], (8, 128))
            value = jnp.take_along_axis(row, index & 127, axis=1, mode="promise_in_bounds")
            found = jnp.where(index >> 7 == i, value, found)
        return [
            (found[2 * i:2 * i + 1] ^ found[2 * i + 1:2 * i + 2]).astype(F32) for i in range(4)
        ]

    def column(row):
        return jnp.broadcast_to(row, (128, 128)).T

    def select_integrals():
        bras, kets = irreps(bra), irreps(ket)
        load.wait()
        for i in range(4):
            bra_irrep = column(bras[i])
            for j in range(4):
                p, q = pl.ds(i * 128, 128), pl.ds(j * 128, 128)
                turned = jnp.where(bra_irrep == kets[j], ints_v[p, q], 0.0).T
                top = turned.astype(BF16)
                w_high[q, p] = top
                w_low[q, p] = (turned - top.astype(F32)).astype(BF16)

    def place_rows():
        place_v[...] = jnp.zeros((16, 128), jnp.int32)
        u = lax.broadcasted_iota(jnp.int32, (128, 128), 0)
        lane = lax.broadcasted_iota(jnp.int32, (128, 128), 1)
        src_x, src_y, src_c = (u >> 2) & 3, ((u >> 4) & 1) * 2 + (u >> 6), (u >> 5) & 1
        fixed = ((src_x * NY + src_y) * CHUNK + src_c) * 4 + (u & 3)

        @pl.loop(0, NZ)
        def _(j):
            dz = (z + NZ - j) % NZ
            k = jnp.where(dz == 0, 0, jnp.where(dz <= 8, 2 * dz - 1, 2 * (NZ - dz)))
            spot = fixed + (k // STEPS * CHUNK_ROWS + k % STEPS * 8)
            pair = column(slots[pl.ds(j, 1), :].astype(F32)).astype(jnp.int32)
            for i in range(16):
                hit = jnp.where(pair == lane + i * 128, spot, 0)
                place_v[i:i + 1, :] += jnp.sum(hit, axis=0, keepdims=True)

        copy = pltpu.make_async_copy(place_v, place, sem_place)
        copy.start()
        copy.wait()

    def span(g):
        return pl.ds(g * CHUNK, CHUNK)

    def row_y(d):
        return (y + NY - d) % NY

    def row_x(d):
        return (x + d) % NX

    def send_x(ref, sems):
        remote(ref, ref, s_x, sems[0], right).start()
        remote(ref, ref, s_x, sems[1], left).start()

    def relay(ref, sem, target):
        remote(ref, ref, s_r, sem, target).start()

    def send_y(g, col):
        for d in (1, 3):
            remote(
                other.at[row_x(col), span(g)], every.at[row_x(col), y, span(g)], s_y,
                r_y.at[g, col, d], device(z, (y + d) % NY, x, c),
            ).start()

    def step_own(g):
        ref = every.at[x, y, span(g)]
        wait_bytes(ref, r_own.at[g])
        remote(ref, ref, s_w, r_y.at[g, 0, 2], device(z, (y + 2) % NY, x, c)).start()
        send_x(ref, (r_x.at[g, 0, 0], r_x.at[g, 1, 0]))

    def step_oth(g):
        ref = other.at[x, span(g)]
        wait_bytes(ref, r_oth.at[g])
        send_x(ref, (r_ox.at[g, 0], r_ox.at[g, 1]))
        send_y(g, 0)

    def step_yown(g):
        ref = every.at[x, row_y(2), span(g)]
        wait_bytes(ref, r_y.at[g, 0, 2])
        send_x(ref, (r_x.at[g, 0, 2], r_x.at[g, 1, 2]))

    def step_ownl(g):
        ref = every.at[row_x(3), y, span(g)]
        wait_bytes(ref, r_x.at[g, 0, 0])
        relay(ref, r_r.at[g, 0], right)

    def step_ownr(g):
        wait_bytes(every.at[row_x(1), y, span(g)], r_x.at[g, 1, 0])

    def step_d2l(g):
        wait_bytes(every.at[row_x(3), row_y(2), span(g)], r_x.at[g, 0, 2])

    def step_d2r(g):
        ref = every.at[row_x(1), row_y(2), span(g)]
        wait_bytes(ref, r_x.at[g, 1, 2])
        relay(ref, r_r.at[g, 2], left)

    def step_othl(g):
        ref = other.at[row_x(3), span(g)]
        wait_bytes(ref, r_ox.at[g, 0])
        if g % 2:
            relay(ref, r_ro.at[g], right)
        send_y(g, 3)

    def step_othr(g):
        ref = other.at[row_x(1), span(g)]
        wait_bytes(ref, r_ox.at[g, 1])
        if g % 2 == 0:
            relay(ref, r_ro.at[g], left)
        send_y(g, 1)

    def step_oth2(g):
        wait_bytes(other.at[row_x(2), span(g)], r_ro.at[g])
        send_y(g, 2)

    def step_dot(g):
        for d in (0, 2):
            wait_bytes(every.at[row_x(2), row_y(d), span(g)], r_r.at[g, d])
        for col in (0, 1, 3, 2):
            for d in (1, 3):
                wait_bytes(every.at[row_x(col), row_y(d), span(g)], r_y.at[g, col, d])

        for xx in range(NX):
            for yy in range(NY):
                value = every[xx, yy, g * CHUNK:(g + 1) * CHUNK].reshape(CHUNK * 4, Q)
                top = value.astype(BF16)
                rows = pl.ds((xx * NY + yy) * CHUNK * 4, CHUNK * 4)
                high[rows, :] = top
                low[rows, :] = (value - top.astype(F32)).astype(BF16)
        result = jnp.dot(high[...], w_high[...], preferred_element_type=F32)
        result += jnp.dot(high[...], w_low[...], preferred_element_type=F32)
        result += jnp.dot(low[...], w_high[...], preferred_element_type=F32)
        part[pl.ds(g * CHUNK_ROWS, CHUNK_ROWS)] = result.reshape(CHUNK_ROWS, 4, 128)

    steps = {
        "own": step_own, "oth": step_oth, "yown": step_yown, "ownL": step_ownl, "ownR": step_ownr,
        "d2L": step_d2l, "d2R": step_d2r, "othL": step_othl, "othR": step_othr, "oth2": step_oth2,
        "dot": step_dot,
    }
    for name, g in ORDER:
        if name == "select":
            select_integrals()
        elif name == "place":
            place_rows()
        else:
            steps[name](g)

    def arm_of(t):
        return (0, 8) if t == 0 else ((t + 1) % 2, 7 - (t - 1) // 2)

    def target_z(t):
        arm, d = arm_of(t)
        return (z + (NZ - d if arm else d)) % NZ

    def sources(t):
        arm, d = arm_of(t)
        if t == 15:
            return [(0, 1), (1, 1)]
        top = 7 if arm else 8
        return [(arm, e) for e in (d + 1, d + 2) if d % 2 and e <= top and (e == d + 1 or e % 2)]

    def receiver(t):
        arm, d = arm_of(t)
        hops = 2 if d % 2 and d > 1 else 1
        return device((z + (NZ - hops if arm else hops)) % NZ, y, x, c)

    def gather(t, half, core, first, count, use):
        base = target_z(t) * 128 + half * 64 + core * 32 + first

        @pl.loop(0, count, unroll=8)
        def _(i):
            use(i, part[place[base // 128, base % 128 + i]])

    partner_core = device(z, y, x, 1 - c)
    partner_y = device(z, y + 1 - 2 * parity, x, c)

    def step_gather(t):
        for half in range(2):
            def put(i, row):
                core_out[t, half, i] = row
            gather(t, half, 1 - c, 0, BLOCK, put)
        remote(core_out.at[t], core_in.at[t], s_c, r_c.at[t], partner_core).start()

    def piece(i):
        return pl.ds(i * PIECE, PIECE)

    def step_core(t):
        wait_bytes(core_in.at[t], r_c.at[t])

        def put_out(i, row):
            y_out[t, i] = row + core_in[t, 1 - parity, i]
        gather(t, 1 - parity, c, 0, NARROW, put_out)
        for i in range(PIECES):
            remote(y_out.at[t, piece(i)], y_in.at[t, piece(i)], s_s, r_s.at[t, i], partner_y).start()

        def put_keep(i, row):
            y_keep[t, i] = row + core_in[t, parity, i]
        gather(t, parity, c, 0, NARROW, put_keep)
        if WIDE:
            for half in range(2):
                def put_wide(i, row):
                    wide[t, half, i] = row + core_in[t, half, NARROW + i]
                gather(t, half, c, NARROW, WIDE, put_wide)

    def finish(value, first):
        row = lax.broadcasted_iota(jnp.int32, value.shape, 0) + (cd * BLOCK + first)
        return jnp.where(row < PAIRS, value, 0.0)

    def step_sum(t, i):
        rows = piece(i)
        wait_bytes(y_in.at[t, rows], r_s.at[t, i])
        value = y_keep[t, rows] + y_in[t, rows]
        for arm, d in sources(t):
            wait_bytes(sum_in.at[arm, d - 1, rows], r_sum.at[arm, d - 1, i])
            value = value + sum_in[arm, d - 1, rows]
        if t == 15:
            out[rows] = finish(value, i * PIECE)
            return
        arm, d = arm_of(t)
        sum_out[t, rows] = value
        remote(sum_out.at[t, rows], sum_in.at[arm, d - 1, rows], s_sum, r_sum.at[arm, d - 1, i], receiver(t)).start()

    def step_wide(t):
        value = wide[t]
        for arm, d in sources(t):
            wait_bytes(wide_in.at[arm, d - 1], r_wide.at[arm, d - 1])
            value = value + wide_in[arm, d - 1]
        wide_out[t] = value
        if t == 15:
            remote(wide_out.at[15, 1 - parity], y_last, s_last, r_last, partner_y).start()
            return
        arm, d = arm_of(t)
        remote(wide_out.at[t], wide_in.at[arm, d - 1], s_wide, r_wide.at[arm, d - 1], receiver(t)).start()

    for name, t, i in SUMS:
        if name == "gather":
            step_gather(t)
        elif name == "core":
            step_core(t)
        elif name == "sum":
            step_sum(t, i)
        else:
            step_wide(t)
    if WIDE:
        wait_bytes(y_last, r_last)
        out[NARROW:BLOCK] = finish(wide_out[15, parity] + y_last[...], NARROW)

    wait_bytes(every.at[0, 0, pl.ds(0, 31)], s_z)
    wait_bytes(every.at[0, 0, pl.ds(0, 31)], s_z)
    for sem, units in ((s_w, 1), (s_y, 8), (s_x, 6), (s_r, 3)):
        for _ in range(units):
            wait_bytes(every.at[0, 0], sem)
    wait_bytes(core_in, s_c)
    wait_bytes(y_in, s_s)
    wait_bytes(sum_out.at[pl.ds(0, 15)], s_sum)
    if WIDE:
        wait_bytes(wide_out.at[pl.ds(0, 15)], s_wide)
        wait_bytes(y_last, s_last)


def on_device(amplitudes, integrals, orbital_irrep, bra_pairs, ket_pairs, slot_pair):
    table = jnp.pad(orbital_irrep, (0, 16 * 128 - orbital_irrep.shape[0])).reshape(16, 128)
    dma = pltpu.SemaphoreType.DMA
    result = pl.pallas_call(
        kernel,
        out_shape=jax.ShapeDtypeStruct((BLOCK, 4, 128), F32),
        in_specs=[
            pl.BlockSpec(memory_space=pl.ANY),
            pl.BlockSpec(memory_space=pl.ANY),
            pl.BlockSpec(memory_space=pltpu.VMEM),
            pl.BlockSpec(memory_space=pltpu.VMEM),
            pl.BlockSpec(memory_space=pltpu.VMEM),
            pl.BlockSpec(memory_space=pltpu.VMEM),
        ],
        out_specs=pl.BlockSpec(memory_space=pltpu.VMEM),
        scratch_shapes=[
            pltpu.VMEM((NX, NY, SLAB, 4, Q), F32),
            pltpu.VMEM((NX, SLAB, 4, Q), F32),
            pltpu.VMEM((CHUNK_ROWS, Q), BF16),
            pltpu.VMEM((CHUNK_ROWS, Q), BF16),
            pltpu.VMEM((Q, N), BF16),
            pltpu.VMEM((Q, N), BF16),
            pltpu.VMEM((N, Q), F32),
            pltpu.VMEM((SLOTS, 4, 128), F32),
            pltpu.VMEM((16, 128), jnp.int32),
            pltpu.SMEM((16, 128), jnp.int32),
            pltpu.VMEM((16, 2, BLOCK, 4, 128), F32),
            pltpu.VMEM((16, 2, BLOCK, 4, 128), F32),
            pltpu.VMEM((16, NARROW, 4, 128), F32),
            pltpu.VMEM((16, NARROW, 4, 128), F32),
            pltpu.VMEM((16, NARROW, 4, 128), F32),
            pltpu.VMEM((max(WIDE, 1), 4, 128), F32),
            pltpu.VMEM((16, 2, max(WIDE, 1), 4, 128), F32),
            pltpu.VMEM((16, NARROW, 4, 128), F32),
            pltpu.VMEM((2, 8, NARROW, 4, 128), F32),
            pltpu.VMEM((16, 2, max(WIDE, 1), 4, 128), F32),
            pltpu.VMEM((2, 8, 2, max(WIDE, 1), 4, 128), F32),
            dma, dma,
            dma, dma((CHUNKS,)), dma((CHUNKS,)),
            dma, dma, dma((CHUNKS, 4, 4)),
            dma, dma((CHUNKS, 2, 4)), dma((CHUNKS, 2)),
            dma, dma((CHUNKS, 4)), dma((CHUNKS,)),
            dma, dma((16,)),
            dma, dma((16, PIECES)),
            dma, dma((2, 8, PIECES)),
            dma, dma((2, 8)),
            dma, dma,
        ],
        compiler_params=pltpu.CompilerParams(
            collective_id=0, has_side_effects=True, vmem_limit_bytes=60 << 20
        ),
        name="ladder",
    )(amplitudes, integrals, table, bra_pairs, ket_pairs, slot_pair.reshape(16, 128))
    return result.reshape(BLOCK, N)


def solution(mesh):
    in_specs = (P(("cd", "ab"), None), P("ab", "cd"), P(), P(None, "ab"), P(None, "cd"), P())
    out_specs = P("cd", "ab")
    return jax.shard_map(
        on_device, mesh=mesh, in_specs=in_specs, out_specs=out_specs, check_vma=False
    )
```

```python
import jax
import jax.numpy as jnp
from jax import lax
from jax.experimental import pallas as pl
from jax.experimental.pallas import tpu as pltpu
from jax.sharding import PartitionSpec as P

PAIRS = 1830
SLOTS = 2048
NZ, NY, NX, NC = 16, 4, 4, 2
Q = 512
N = 512
SLAB = NZ * NC
CHUNKS = 8
STEPS = NZ // CHUNKS
CHUNK = SLAB // CHUNKS
CHUNK_ROWS = CHUNK * 4 * NX * NY
TABLE = 13
BLOCK = 32
ORDER = (
    ("select", 0), ("own", 0), ("oth", 0), ("far", 0), ("own", 1), ("oth", 1), ("ownL", 0), ("ownR", 0), ("othL", 0),
    ("othR", 0), ("yown", 0), ("ownL", 1), ("ownR", 1), ("own", 2), ("oth", 2), ("othL", 1), ("othR", 1),
    ("yown", 1), ("oth2", 0), ("d2L", 0), ("place", 0), ("d2R", 0), ("own", 3), ("oth", 3), ("ownR", 2),
    ("ownL", 2), ("othR", 2), ("yown", 2), ("othL", 2), ("d2R", 1), ("oth2", 1), ("d2L", 1), ("own", 4),
    ("oth", 4), ("ownL", 3), ("ownR", 3), ("othL", 3), ("yown", 3), ("othR", 3), ("oth2", 2), ("d2L", 2),
    ("dot", 0), ("d2R", 2), ("ownL", 4), ("own", 5), ("oth", 5), ("othL", 4), ("ownR", 4), ("yown", 4),
    ("othR", 4), ("oth2", 3), ("d2R", 3), ("d2L", 3), ("dot", 1), ("own", 6), ("oth", 6), ("ownR", 5),
    ("ownL", 5), ("othR", 5), ("othL", 5), ("yown", 5), ("d2R", 4), ("d2L", 4), ("own", 7), ("oth", 7),
    ("oth2", 4), ("ownL", 6), ("othL", 6), ("ownR", 6), ("dot", 2), ("othR", 6), ("oth2", 5), ("yown", 6),
    ("d2R", 5), ("d2L", 5), ("dot", 3), ("ownL", 7), ("ownR", 7), ("othL", 7), ("othR", 7), ("yown", 7),
    ("oth2", 6), ("d2L", 6), ("d2R", 6), ("dot", 4), ("oth2", 7), ("d2R", 7), ("dot", 5), ("d2L", 7),
    ("dot", 6), ("dot", 7),
)
WIDE = 4
NARROW = BLOCK - WIDE
PIECES = 2
PIECE = NARROW // PIECES
SUMS = (
    ("gather", 0, 0), ("gather", 1, 0), ("gather", 2, 0), ("gather", 3, 0), ("gather", 4, 0),
    ("gather", 5, 0), ("gather", 6, 0), ("gather", 7, 0), ("core", 0, 0), ("wide", 0, 0), ("core", 1, 0),
    ("core", 2, 0), ("wide", 2, 0), ("core", 3, 0), ("wide", 3, 0), ("core", 4, 0), ("wide", 4, 0),
    ("core", 5, 0), ("core", 6, 0), ("core", 7, 0), ("wide", 7, 0), ("wide", 1, 0), ("sum", 0, 0),
    ("sum", 0, 1), ("gather", 8, 0), ("gather", 9, 0), ("wide", 6, 0), ("sum", 2, 0), ("gather", 10, 0),
    ("gather", 11, 0), ("sum", 2, 1), ("gather", 12, 0), ("sum", 3, 0), ("gather", 13, 0), ("sum", 3, 1),
    ("core", 8, 0), ("wide", 8, 0), ("core", 9, 0), ("sum", 4, 0), ("sum", 1, 0), ("wide", 5, 0),
    ("core", 10, 0), ("sum", 4, 1), ("core", 11, 0), ("wide", 11, 0), ("sum", 1, 1), ("core", 12, 0),
    ("wide", 12, 0), ("core", 13, 0), ("wide", 10, 0), ("sum", 7, 0), ("gather", 14, 0), ("sum", 6, 0),
    ("sum", 7, 1), ("gather", 15, 0), ("sum", 6, 1), ("sum", 8, 0), ("sum", 5, 0), ("sum", 8, 1),
    ("wide", 13, 0), ("wide", 9, 0), ("core", 14, 0), ("wide", 14, 0), ("core", 15, 0), ("sum", 5, 1),
    ("sum", 11, 0), ("sum", 11, 1), ("sum", 12, 0), ("sum", 9, 0), ("sum", 10, 0), ("sum", 12, 1),
    ("sum", 10, 1), ("wide", 15, 0), ("sum", 13, 0), ("sum", 9, 1), ("sum", 14, 0), ("sum", 13, 1),
    ("sum", 14, 1), ("sum", 15, 0), ("sum", 15, 1),
)
NEXT = (-1, 0, 1, 0, 3, 3, 5, 5, 7)
MESH = pl.DeviceIdType.MESH
F32 = jnp.float32
BF16 = jnp.bfloat16


def device(z, y, x, c):
    return {"cd": z * 4 + (y % 2) * 2 + c, "ab": (y // 2) * 4 + x}


def remote(src, dst, send, recv, target):
    return pltpu.make_async_remote_copy(
        src_ref=src, dst_ref=dst, send_sem=send, recv_sem=recv,
        device_id=target, device_id_type=MESH,
    )


def wait_bytes(ref, sem):
    pltpu.make_async_copy(ref, ref, sem).wait()


def offset_of(k):
    odd = k % 2
    return odd * ((k + 1) // 2) + (1 - odd) * ((NZ - k // 2) % NZ)


def kernel(
    amp_hbm, ints, table, bra, ket, slots, out,
    every, other, high, low, w_high, w_low, ints_v, part, place_v, place,
    core_out, core_in, y_out, y_keep, y_in, y_last, wide, sum_out, sum_in, wide_out, wide_in,
    amp, sem_amp, sem_two, sem_four, sem_ints, sem_place, s_z, r_own, r_oth, s_w, s_y, r_y, s_x, r_x, r_ox, s_r, r_r, r_ro,
    s_c, r_c, s_s, r_s, s_sum, r_sum, s_wide, r_wide, s_last, r_last,
):
    cd, ab = lax.axis_index("cd"), lax.axis_index("ab")
    z, c, x = cd // 4, cd % 2, ab % 4
    parity = (cd // 2) % 2
    y = (ab // 4) * 2 + parity

    barrier = pltpu.get_barrier_semaphore()
    right, left = device(z, y, (x + 1) % NX, c), device(z, y, (x + 3) % NX, c)
    greet = [device(z, y, x, 1 - c), right, left]
    greet += [device(z, (y + d) % NY, x, c) for d in (1, 2, 3)]
    greet += [device((z + d) % NZ, y, x, (c + dc) % 2) for d in (1, 15, 2, 14) for dc in range(NC)]
    for target in greet:
        pl.semaphore_signal(barrier, inc=1, device_id=target, device_id_type=MESH)
    load = pltpu.make_async_copy(ints, ints_v, sem_ints)
    load.start()
    stage = pltpu.make_async_copy(amp_hbm, amp, sem_amp)
    stage.start()
    pl.semaphore_wait(barrier, len(greet))

    def vouch(sem, d):
        for zz in ((z + d) % NZ, (z + NZ - d) % NZ):
            pl.semaphore_signal(sem, inc=1, device_id=device(zz, y, x, c), device_id_type=MESH)

    vouch(sem_two, 2)
    stage.wait()

    def slab(zz, half, core):
        return amp.at[:, pl.ds(pl.multiple_of(zz * 2048 + half * 1024 + core * 512, 512), Q)]

    def send_z(k, dc):
        zz, cc = (z + offset_of(k)) % NZ, (c + dc) % 2
        entry, g, target = k * 2 + c, k // STEPS, device(zz, y, x, cc)
        remote(slab(zz, 1 - parity, cc), other.at[x, entry], s_z, r_oth.at[g], target).start()
        remote(slab(zz, parity, cc), every.at[x, y, entry], s_z, r_own.at[g], target).start()

    pltpu.make_async_copy(slab(z, 1 - parity, c), other.at[x, c], r_oth.at[0]).start()
    pltpu.make_async_copy(slab(z, parity, c), every.at[x, y, c], r_own.at[0]).start()
    send_z(0, 1)

    def send_range(first, last):
        @pl.loop(first, last)
        def _(k):
            send_z(k, 0)
            send_z(k, 1)

    send_range(1, 5)
    pl.semaphore_wait(sem_two, 2)
    vouch(sem_four, 4)
    send_range(5, 9)

    def send_far():
        pl.semaphore_wait(sem_four, 2)
        send_range(9, NZ)

    def irreps(pairs):
        index = jnp.concatenate([pairs[:, i * 128:(i + 1) * 128] for i in range(4)], axis=0)
        found = jnp.zeros((8, 128), jnp.int32)
        for i in range(TABLE):
            if (i + 1) * 128 <= table.shape[0]:
                row = table[pl.ds(i * 128, 128)].reshape(1, 128)
            else:
                rest = table[pl.ds(i * 128, table.shape[0] - i * 128)].reshape(1, table.shape[0] - i * 128)
                row = jnp.concatenate([rest, jnp.zeros((1, 128 - rest.shape[1]), jnp.int32)], axis=1)
            row = jnp.broadcast_to(row, (8, 128))
            value = jnp.take_along_axis(row, index & 127, axis=1, mode="promise_in_bounds")
            found = jnp.where(index >> 7 == i, value, found)
        return [
            (found[2 * i:2 * i + 1] ^ found[2 * i + 1:2 * i + 2]).astype(F32) for i in range(4)
        ]

    def column(row):
        return jnp.broadcast_to(row, (128, 128)).T

    def select_integrals():
        bras, kets = irreps(bra), irreps(ket)
        load.wait()
        for i in range(4):
            bra_irrep = column(bras[i])
            for j in range(4):
                p, q = pl.ds(i * 128, 128), pl.ds(j * 128, 128)
                turned = jnp.where(bra_irrep == kets[j], ints_v[p, q], 0.0).T
                top = turned.astype(BF16)
                w_high[q, p] = top
                w_low[q, p] = (turned - top.astype(F32)).astype(BF16)

    def place_rows():
        place_v[...] = jnp.zeros((16, 128), jnp.int32)
        u = lax.broadcasted_iota(jnp.int32, (128, 128), 0)
        lane = lax.broadcasted_iota(jnp.int32, (128, 128), 1)
        src_x, src_y, src_c = (u >> 2) & 3, ((u >> 4) & 1) * 2 + (u >> 6), (u >> 5) & 1
        fixed = ((src_x * NY + src_y) * CHUNK + src_c) * 4 + (u & 3)

        @pl.loop(0, NZ)
        def _(j):
            dz = (z + NZ - j) % NZ
            k = jnp.where(dz == 0, 0, jnp.where(dz <= 8, 2 * dz - 1, 2 * (NZ - dz)))
            spot = fixed + (k // STEPS * CHUNK_ROWS + k % STEPS * 8)
            pair = column(slots[pl.ds(j, 1), :].astype(F32)).astype(jnp.int32)
            for i in range(16):
                hit = jnp.where(pair == lane + i * 128, spot, 0)
                place_v[i:i + 1, :] += jnp.sum(hit, axis=0, keepdims=True)

        copy = pltpu.make_async_copy(place_v, place, sem_place)
        copy.start()
        copy.wait()

    def span(g):
        return pl.ds(g * CHUNK, CHUNK)

    def row_y(d):
        return (y + NY - d) % NY

    def row_x(d):
        return (x + d) % NX

    def send_x(ref, sems):
        remote(ref, ref, s_x, sems[0], right).start()
        remote(ref, ref, s_x, sems[1], left).start()

    def relay(ref, sem, target):
        remote(ref, ref, s_r, sem, target).start()

    def send_y(g, col):
        for d in (1, 3):
            remote(
                other.at[row_x(col), span(g)], every.at[row_x(col), y, span(g)], s_y,
                r_y.at[g, col, d], device(z, (y + d) % NY, x, c),
            ).start()

    def step_own(g):
        ref = every.at[x, y, span(g)]
        wait_bytes(ref, r_own.at[g])
        remote(ref, ref, s_w, r_y.at[g, 0, 2], device(z, (y + 2) % NY, x, c)).start()
        send_x(ref, (r_x.at[g, 0, 0], r_x.at[g, 1, 0]))

    def step_oth(g):
        ref = other.at[x, span(g)]
        wait_bytes(ref, r_oth.at[g])
        send_x(ref, (r_ox.at[g, 0], r_ox.at[g, 1]))
        send_y(g, 0)

    def step_yown(g):
        ref = every.at[x, row_y(2), span(g)]
        wait_bytes(ref, r_y.at[g, 0, 2])
        send_x(ref, (r_x.at[g, 0, 2], r_x.at[g, 1, 2]))

    def step_ownl(g):
        ref = every.at[row_x(3), y, span(g)]
        wait_bytes(ref, r_x.at[g, 0, 0])
        relay(ref, r_r.at[g, 0], right)

    def step_ownr(g):
        wait_bytes(every.at[row_x(1), y, span(g)], r_x.at[g, 1, 0])

    def step_d2l(g):
        wait_bytes(every.at[row_x(3), row_y(2), span(g)], r_x.at[g, 0, 2])

    def step_d2r(g):
        ref = every.at[row_x(1), row_y(2), span(g)]
        wait_bytes(ref, r_x.at[g, 1, 2])
        relay(ref, r_r.at[g, 2], left)

    def step_othl(g):
        ref = other.at[row_x(3), span(g)]
        wait_bytes(ref, r_ox.at[g, 0])
        if g % 2:
            relay(ref, r_ro.at[g], right)
        send_y(g, 3)

    def step_othr(g):
        ref = other.at[row_x(1), span(g)]
        wait_bytes(ref, r_ox.at[g, 1])
        if g % 2 == 0:
            relay(ref, r_ro.at[g], left)
        send_y(g, 1)

    def step_oth2(g):
        wait_bytes(other.at[row_x(2), span(g)], r_ro.at[g])
        send_y(g, 2)

    def step_dot(g):
        for d in (0, 2):
            wait_bytes(every.at[row_x(2), row_y(d), span(g)], r_r.at[g, d])
        for col in (0, 1, 3, 2):
            for d in (1, 3):
                wait_bytes(every.at[row_x(col), row_y(d), span(g)], r_y.at[g, col, d])

        for xx in range(NX):
            for yy in range(NY):
                value = every[xx, yy, g * CHUNK:(g + 1) * CHUNK].reshape(CHUNK * 4, Q)
                top = value.astype(BF16)
                rows = pl.ds((xx * NY + yy) * CHUNK * 4, CHUNK * 4)
                high[rows, :] = top
                low[rows, :] = (value - top.astype(F32)).astype(BF16)
        result = jnp.dot(high[...], w_high[...], preferred_element_type=F32)
        result += jnp.dot(high[...], w_low[...], preferred_element_type=F32)
        result += jnp.dot(low[...], w_high[...], preferred_element_type=F32)
        part[pl.ds(g * CHUNK_ROWS, CHUNK_ROWS)] = result.reshape(CHUNK_ROWS, 4, 128)

    steps = {
        "own": step_own, "oth": step_oth, "yown": step_yown, "ownL": step_ownl, "ownR": step_ownr,
        "d2L": step_d2l, "d2R": step_d2r, "othL": step_othl, "othR": step_othr, "oth2": step_oth2,
        "dot": step_dot,
    }
    for name, g in ORDER:
        if name == "far":
            send_far()
        elif name == "select":
            select_integrals()
        elif name == "place":
            place_rows()
        else:
            steps[name](g)

    def arm_of(t):
        return (0, 8) if t == 0 else ((t + 1) % 2, 7 - (t - 1) // 2)

    def target_z(t):
        arm, d = arm_of(t)
        return (z + (NZ - d if arm else d)) % NZ

    def sources(t):
        arm, d = arm_of(t)
        arms = (0, 1) if t == 15 else (arm,)
        return [(a, e) for a in arms for e in range(1, 8 if a else 9) if NEXT[e] == d]

    def receiver(t):
        arm, d = arm_of(t)
        hops = d - NEXT[d]
        return device((z + (NZ - hops if arm else hops)) % NZ, y, x, c)

    def holds_rows(t, half):
        return target_z(t) * 128 + half * 64 < PAIRS

    def gather(t, half, core, first, count, use):
        base = target_z(t) * 128 + half * 64 + core * 32 + first

        @pl.loop(0, count, unroll=8)
        def _(i):
            use(i, part[place[base // 128, base % 128 + i]])

    partner_core = device(z, y, x, 1 - c)
    partner_y = device(z, y + 1 - 2 * parity, x, c)

    def step_gather(t):
        @pl.when(holds_rows(t, 0))
        def _():
            for half in range(2):
                def put(i, row):
                    core_out[t, half, i] = row
                gather(t, half, 1 - c, 0, BLOCK, put)
            remote(core_out.at[t], core_in.at[t], s_c, r_c.at[t], partner_core).start()

    def piece(i):
        return pl.ds(i * PIECE, PIECE)

    def step_core(t):
        @pl.when(holds_rows(t, 0))
        def _():
            wait_bytes(core_in.at[t], r_c.at[t])

        @pl.when(holds_rows(t, 1 - parity))
        def _():
            def put_out(i, row):
                y_out[t, i] = row + core_in[t, 1 - parity, i]
            gather(t, 1 - parity, c, 0, NARROW, put_out)
            for i in range(PIECES):
                remote(y_out.at[t, piece(i)], y_in.at[t, piece(i)], s_s, r_s.at[t, i], partner_y).start()

        @pl.when(holds_rows(t, 0))
        def _():
            def put_keep(i, row):
                y_keep[t, i] = row + core_in[t, parity, i]
            gather(t, parity, c, 0, NARROW, put_keep)
            for half in range(2):
                def put_wide(i, row):
                    wide[t, half, i] = row + core_in[t, half, NARROW + i]
                gather(t, half, c, NARROW, WIDE, put_wide)

    def finish(value, first):
        row = lax.broadcasted_iota(jnp.int32, value.shape, 0) + (cd * BLOCK + first)
        return jnp.where(row < PAIRS, value, 0.0)

    def step_sum(t, i):
        rows = piece(i)

        @pl.when(holds_rows(t, parity))
        def _():
            wait_bytes(y_in.at[t, rows], r_s.at[t, i])
            value = y_keep[t, rows] + y_in[t, rows]
            for arm, d in sources(t):
                wait_bytes(sum_in.at[arm, d - 1, rows], r_sum.at[arm, d - 1, i])
                value = value + sum_in[arm, d - 1, rows]
            if t == 15:
                out[rows] = finish(value, i * PIECE)
                return
            arm, d = arm_of(t)
            sum_out[t, rows] = value
            remote(
                sum_out.at[t, rows], sum_in.at[arm, d - 1, rows], s_sum,
                r_sum.at[arm, d - 1, i], receiver(t),
            ).start()

    def step_wide(t):
        @pl.when(holds_rows(t, 0))
        def _():
            value = wide[t]
            for arm, d in sources(t):
                wait_bytes(wide_in.at[arm, d - 1], r_wide.at[arm, d - 1])
                value = value + wide_in[arm, d - 1]
            wide_out[t] = value
            if t == 15:
                remote(wide_out.at[15, 1 - parity], y_last, s_last, r_last, partner_y).start()
                return
            arm, d = arm_of(t)
            remote(
                wide_out.at[t], wide_in.at[arm, d - 1], s_wide, r_wide.at[arm, d - 1], receiver(t)
            ).start()

    @pl.when(cd * BLOCK >= PAIRS)
    def _():
        out[...] = jnp.zeros(out.shape, F32)

    for name, t, i in SUMS:
        if name == "gather":
            step_gather(t)
        elif name == "core":
            step_core(t)
        elif name == "sum":
            step_sum(t, i)
        else:
            step_wide(t)

    @pl.when(holds_rows(15, 0))
    def _():
        wait_bytes(y_last, r_last)
        out[NARROW:BLOCK] = finish(wide_out[15, parity] + y_last[...], NARROW)

    wait_bytes(every.at[0, 0, pl.ds(0, 31)], s_z)
    wait_bytes(every.at[0, 0, pl.ds(0, 31)], s_z)
    for sem, units in ((s_w, 1), (s_y, 8), (s_x, 6), (s_r, 3)):
        for _ in range(units):
            wait_bytes(every.at[0, 0], sem)
    for t in range(16):
        @pl.when(holds_rows(t, 0))
        def _():
            wait_bytes(core_in.at[t], s_c)
            wait_bytes(wide_out.at[t] if t < 15 else y_last, s_wide if t < 15 else s_last)

        @pl.when(holds_rows(t, 1 - parity))
        def _():
            wait_bytes(y_in.at[t], s_s)

        if t < 15:
            @pl.when(holds_rows(t, parity))
            def _():
                wait_bytes(sum_out.at[t], s_sum)


def on_device(amplitudes, integrals, orbital_irrep, bra_pairs, ket_pairs, slot_pair):
    dma = pltpu.SemaphoreType.DMA
    result = pl.pallas_call(
        kernel,
        out_shape=jax.ShapeDtypeStruct((BLOCK, 4, 128), F32),
        in_specs=[
            pl.BlockSpec(memory_space=pl.ANY),
            pl.BlockSpec(memory_space=pl.ANY),
            pl.BlockSpec(memory_space=pltpu.VMEM),
            pl.BlockSpec(memory_space=pltpu.VMEM),
            pl.BlockSpec(memory_space=pltpu.VMEM),
            pl.BlockSpec(memory_space=pltpu.VMEM),
        ],
        out_specs=pl.BlockSpec(memory_space=pltpu.VMEM),
        scratch_shapes=[
            pltpu.VMEM((NX, NY, SLAB, 4, Q), F32),
            pltpu.VMEM((NX, SLAB, 4, Q), F32),
            pltpu.VMEM((CHUNK_ROWS, Q), BF16),
            pltpu.VMEM((CHUNK_ROWS, Q), BF16),
            pltpu.VMEM((Q, N), BF16),
            pltpu.VMEM((Q, N), BF16),
            pltpu.VMEM((N, Q), F32),
            pltpu.VMEM((SLOTS, 4, 128), F32),
            pltpu.VMEM((16, 128), jnp.int32),
            pltpu.SMEM((16, 128), jnp.int32),
            pltpu.VMEM((16, 2, BLOCK, 4, 128), F32),
            pltpu.VMEM((16, 2, BLOCK, 4, 128), F32),
            pltpu.VMEM((16, NARROW, 4, 128), F32),
            pltpu.VMEM((16, NARROW, 4, 128), F32),
            pltpu.VMEM((16, NARROW, 4, 128), F32),
            pltpu.VMEM((max(WIDE, 1), 4, 128), F32),
            pltpu.VMEM((16, 2, max(WIDE, 1), 4, 128), F32),
            pltpu.VMEM((16, NARROW, 4, 128), F32),
            pltpu.VMEM((2, 8, NARROW, 4, 128), F32),
            pltpu.VMEM((16, 2, max(WIDE, 1), 4, 128), F32),
            pltpu.VMEM((2, 8, 2, max(WIDE, 1), 4, 128), F32),
            pltpu.VMEM((4, NZ * 2048), F32), dma,
            pltpu.SemaphoreType.REGULAR, pltpu.SemaphoreType.REGULAR,
            dma, dma,
            dma, dma((CHUNKS,)), dma((CHUNKS,)),
            dma, dma, dma((CHUNKS, 4, 4)),
            dma, dma((CHUNKS, 2, 4)), dma((CHUNKS, 2)),
            dma, dma((CHUNKS, 4)), dma((CHUNKS,)),
            dma, dma((16,)),
            dma, dma((16, PIECES)),
            dma, dma((2, 8, PIECES)),
            dma, dma((2, 8)),
            dma, dma,
        ],
        compiler_params=pltpu.CompilerParams(
            collective_id=0, has_side_effects=True, vmem_limit_bytes=60 << 20
        ),
        name="ladder",
    )(amplitudes, integrals, orbital_irrep, bra_pairs, ket_pairs, slot_pair.reshape(16, 128))
    return result.reshape(BLOCK, N)


def solution(mesh):
    in_specs = (P(("cd", "ab"), None), P("ab", "cd"), P(), P(None, "ab"), P(None, "cd"), P())
    out_specs = P("cd", "ab")
    return jax.shard_map(
        on_device, mesh=mesh, in_specs=in_specs, out_specs=out_specs, check_vma=False
    )
```

```python
import jax
import jax.numpy as jnp
from jax import lax
from jax.experimental import pallas as pl
from jax.experimental.pallas import tpu as pltpu
from jax.sharding import PartitionSpec as P

PAIRS = 1830
SLOTS = 2048
NZ, NY, NX, NC = 16, 4, 4, 2
Q = 512
N = 512
SLAB = NZ * NC
CHUNKS = 8
STEPS = NZ // CHUNKS
CHUNK = SLAB // CHUNKS
CHUNK_ROWS = CHUNK * 4 * NX * NY
TABLE = 13
BLOCK = 32
ORDER = (
    ("select", 0), ("own", 0), ("oth", 0), ("far", 0), ("own", 1), ("oth", 1), ("ownL", 0), ("ownR", 0), ("othL", 0),
    ("othR", 0), ("yown", 0), ("ownL", 1), ("ownR", 1), ("own", 2), ("oth", 2), ("othL", 1), ("othR", 1),
    ("yown", 1), ("oth2", 0), ("d2L", 0), ("place", 0), ("d2R", 0), ("own", 3), ("oth", 3), ("ownR", 2),
    ("ownL", 2), ("othR", 2), ("yown", 2), ("othL", 2), ("d2R", 1), ("oth2", 1), ("d2L", 1), ("own", 4),
    ("oth", 4), ("ownL", 3), ("ownR", 3), ("othL", 3), ("yown", 3), ("othR", 3), ("oth2", 2), ("d2L", 2),
    ("dot", 0), ("d2R", 2), ("ownL", 4), ("own", 5), ("oth", 5), ("othL", 4), ("ownR", 4), ("yown", 4),
    ("othR", 4), ("oth2", 3), ("d2R", 3), ("d2L", 3), ("dot", 1), ("own", 6), ("oth", 6), ("ownR", 5),
    ("ownL", 5), ("othR", 5), ("othL", 5), ("yown", 5), ("d2R", 4), ("d2L", 4), ("own", 7), ("oth", 7),
    ("oth2", 4), ("ownL", 6), ("othL", 6), ("ownR", 6), ("dot", 2), ("othR", 6), ("oth2", 5), ("yown", 6),
    ("d2R", 5), ("d2L", 5), ("dot", 3), ("ownL", 7), ("ownR", 7), ("othL", 7), ("othR", 7), ("yown", 7),
    ("oth2", 6), ("d2L", 6), ("d2R", 6), ("dot", 4), ("oth2", 7), ("d2R", 7), ("dot", 5), ("d2L", 7),
    ("dot", 6), ("dot", 7),
)
WIDE = 4
NARROW = BLOCK - WIDE
PIECES = 2
PIECE = NARROW // PIECES
SUMS = (
    ("gather", 0, 0), ("gather", 1, 0), ("gather", 2, 0), ("gather", 3, 0), ("gather", 4, 0),
    ("gather", 5, 0), ("gather", 6, 0), ("gather", 7, 0), ("core", 0, 0), ("wide", 0, 0), ("core", 1, 0),
    ("core", 2, 0), ("wide", 2, 0), ("core", 3, 0), ("wide", 3, 0), ("core", 4, 0), ("wide", 4, 0),
    ("core", 5, 0), ("core", 6, 0), ("core", 7, 0), ("wide", 7, 0), ("wide", 1, 0), ("sum", 0, 0),
    ("sum", 0, 1), ("gather", 8, 0), ("gather", 9, 0), ("wide", 6, 0), ("sum", 2, 0), ("gather", 10, 0),
    ("gather", 11, 0), ("sum", 2, 1), ("gather", 12, 0), ("sum", 3, 0), ("gather", 13, 0), ("sum", 3, 1),
    ("core", 8, 0), ("wide", 8, 0), ("core", 9, 0), ("sum", 4, 0), ("sum", 1, 0), ("wide", 5, 0),
    ("core", 10, 0), ("sum", 4, 1), ("core", 11, 0), ("wide", 11, 0), ("sum", 1, 1), ("core", 12, 0),
    ("wide", 12, 0), ("core", 13, 0), ("wide", 10, 0), ("sum", 7, 0), ("gather", 14, 0), ("sum", 6, 0),
    ("sum", 7, 1), ("gather", 15, 0), ("sum", 6, 1), ("sum", 8, 0), ("sum", 5, 0), ("sum", 8, 1),
    ("wide", 13, 0), ("wide", 9, 0), ("core", 14, 0), ("wide", 14, 0), ("core", 15, 0), ("sum", 5, 1),
    ("sum", 11, 0), ("sum", 11, 1), ("sum", 12, 0), ("sum", 9, 0), ("sum", 10, 0), ("sum", 12, 1),
    ("sum", 10, 1), ("wide", 15, 0), ("sum", 13, 0), ("sum", 9, 1), ("sum", 14, 0), ("sum", 13, 1),
    ("sum", 14, 1), ("sum", 15, 0), ("sum", 15, 1),
)
NEXT = (-1, 0, 1, 0, 3, 3, 5, 5, 7)
MESH = pl.DeviceIdType.MESH
F32 = jnp.float32
BF16 = jnp.bfloat16


def device(z, y, x, c):
    return {"cd": z * 4 + (y % 2) * 2 + c, "ab": (y // 2) * 4 + x}


def remote(src, dst, send, recv, target):
    return pltpu.make_async_remote_copy(
        src_ref=src, dst_ref=dst, send_sem=send, recv_sem=recv,
        device_id=target, device_id_type=MESH,
    )


def wait_bytes(ref, sem):
    pltpu.make_async_copy(ref, ref, sem).wait()


def offset_of(k):
    odd = k % 2
    return odd * ((k + 1) // 2) + (1 - odd) * ((NZ - k // 2) % NZ)


def kernel(
    amp_hbm, ints, table, bra, ket, slots, out,
    every, other, high, low, w_high, w_low, ints_v, part, place_v, place,
    core_out, core_in, y_out, y_keep, y_in, y_last, wide, sum_out, sum_in, wide_out, wide_in,
    amp, sem_amp, sem_two, sem_four, sem_ints, sem_place, s_z, r_own, r_oth, s_w, s_y, r_y, s_x, r_x, r_ox, s_r, r_r, r_ro,
    s_c, r_c, s_s, r_s, s_sum, r_sum, s_wide, r_wide, s_last, r_last,
):
    cd, ab = lax.axis_index("cd"), lax.axis_index("ab")
    z, c, x = cd // 4, cd % 2, ab % 4
    parity = (cd // 2) % 2
    y = (ab // 4) * 2 + parity

    barrier = pltpu.get_barrier_semaphore()
    right, left = device(z, y, (x + 1) % NX, c), device(z, y, (x + 3) % NX, c)
    greet = [device(z, y, x, 1 - c), right, left]
    greet += [device(z, (y + d) % NY, x, c) for d in (1, 2, 3)]
    greet += [device((z + d) % NZ, y, x, (c + dc) % 2) for d in (1, 15, 2, 14) for dc in range(NC)]
    for target in greet:
        pl.semaphore_signal(barrier, inc=1, device_id=target, device_id_type=MESH)
    load = pltpu.make_async_copy(ints, ints_v, sem_ints)
    load.start()
    stage = pltpu.make_async_copy(amp_hbm, amp, sem_amp)
    stage.start()
    pl.semaphore_wait(barrier, len(greet))

    def vouch(sem, d):
        for zz in ((z + d) % NZ, (z + NZ - d) % NZ):
            pl.semaphore_signal(sem, inc=1, device_id=device(zz, y, x, c), device_id_type=MESH)

    vouch(sem_two, 2)
    stage.wait()

    def slab(zz, half, core):
        return amp.at[:, pl.ds(pl.multiple_of(zz * 2048 + half * 1024 + core * 512, 512), Q)]

    def send_z(k, dc):
        zz, cc = (z + offset_of(k)) % NZ, (c + dc) % 2
        entry, g, target = k * 2 + c, k // STEPS, device(zz, y, x, cc)
        remote(slab(zz, 1 - parity, cc), other.at[x, entry], s_z, r_oth.at[g], target).start()
        remote(slab(zz, parity, cc), every.at[x, y, entry], s_z, r_own.at[g], target).start()

    pltpu.make_async_copy(slab(z, 1 - parity, c), other.at[x, c], r_oth.at[0]).start()
    pltpu.make_async_copy(slab(z, parity, c), every.at[x, y, c], r_own.at[0]).start()
    send_z(0, 1)

    def send_range(first, last):
        @pl.loop(first, last)
        def _(k):
            send_z(k, 0)
            send_z(k, 1)

    send_range(1, 5)
    pl.semaphore_wait(sem_two, 2)
    vouch(sem_four, 4)
    send_range(5, 9)

    def send_far():
        pl.semaphore_wait(sem_four, 2)
        send_range(9, NZ)

    def irreps(pairs):
        index = jnp.concatenate([pairs[:, i * 128:(i + 1) * 128] for i in range(4)], axis=0)
        found = jnp.zeros((8, 128), jnp.int32)
        for i in range(TABLE):
            if (i + 1) * 128 <= table.shape[0]:
                row = table[pl.ds(i * 128, 128)].reshape(1, 128)
            else:
                rest = table[pl.ds(i * 128, table.shape[0] - i * 128)].reshape(1, table.shape[0] - i * 128)
                row = jnp.concatenate([rest, jnp.zeros((1, 128 - rest.shape[1]), jnp.int32)], axis=1)
            row = jnp.broadcast_to(row, (8, 128))
            value = jnp.take_along_axis(row, index & 127, axis=1, mode="promise_in_bounds")
            found = jnp.where(index >> 7 == i, value, found)
        return [
            (found[2 * i:2 * i + 1] ^ found[2 * i + 1:2 * i + 2]).astype(F32) for i in range(4)
        ]

    def column(row):
        return jnp.broadcast_to(row, (128, 128)).T

    def select_integrals():
        bras, kets = irreps(bra), irreps(ket)
        load.wait()
        for i in range(4):
            bra_irrep = column(bras[i])
            for j in range(4):
                p, q = pl.ds(i * 128, 128), pl.ds(j * 128, 128)
                turned = jnp.where(bra_irrep == kets[j], ints_v[p, q], 0.0).T
                top = turned.astype(BF16)
                w_high[q, p] = top
                w_low[q, p] = (turned - top.astype(F32)).astype(BF16)

    def place_rows():
        place_v[...] = jnp.zeros((16, 128), jnp.int32)
        u = lax.broadcasted_iota(jnp.int32, (128, 128), 0)
        lane = lax.broadcasted_iota(jnp.int32, (128, 128), 1)
        src_x, src_y, src_c = (u >> 2) & 3, ((u >> 4) & 1) * 2 + (u >> 6), (u >> 5) & 1
        fixed = ((src_x * NY + src_y) * CHUNK + src_c) * 4 + (u & 3)

        @pl.loop(0, NZ)
        def _(j):
            dz = (z + NZ - j) % NZ
            k = jnp.where(dz == 0, 0, jnp.where(dz <= 8, 2 * dz - 1, 2 * (NZ - dz)))
            spot = fixed + (k // STEPS * CHUNK_ROWS + k % STEPS * 8)
            pair = column(slots[pl.ds(j, 1), :].astype(F32)).astype(jnp.int32)
            for i in range(16):
                hit = jnp.where(pair == lane + i * 128, spot, 0)
                place_v[i:i + 1, :] += jnp.sum(hit, axis=0, keepdims=True)

        copy = pltpu.make_async_copy(place_v, place, sem_place)
        copy.start()
        copy.wait()

    def span(g):
        return pl.ds(g * CHUNK, CHUNK)

    def row_y(d):
        return (y + NY - d) % NY

    def row_x(d):
        return (x + d) % NX

    def send_x(ref, sems):
        remote(ref, ref, s_x, sems[0], right).start()
        remote(ref, ref, s_x, sems[1], left).start()

    def relay(ref, sem, target):
        remote(ref, ref, s_r, sem, target).start()

    def send_y(g, col):
        for d in (1, 3):
            remote(
                other.at[row_x(col), span(g)], every.at[row_x(col), y, span(g)], s_y,
                r_y.at[g, col, d], device(z, (y + d) % NY, x, c),
            ).start()

    def step_own(g):
        ref = every.at[x, y, span(g)]
        wait_bytes(ref, r_own.at[g])
        remote(ref, ref, s_w, r_y.at[g, 0, 2], device(z, (y + 2) % NY, x, c)).start()
        send_x(ref, (r_x.at[g, 0, 0], r_x.at[g, 1, 0]))

    def step_oth(g):
        ref = other.at[x, span(g)]
        wait_bytes(ref, r_oth.at[g])
        send_x(ref, (r_ox.at[g, 0], r_ox.at[g, 1]))
        send_y(g, 0)

    def step_yown(g):
        ref = every.at[x, row_y(2), span(g)]
        wait_bytes(ref, r_y.at[g, 0, 2])
        send_x(ref, (r_x.at[g, 0, 2], r_x.at[g, 1, 2]))

    def step_ownl(g):
        ref = every.at[row_x(3), y, span(g)]
        wait_bytes(ref, r_x.at[g, 0, 0])
        relay(ref, r_r.at[g, 0], right)

    def step_ownr(g):
        wait_bytes(every.at[row_x(1), y, span(g)], r_x.at[g, 1, 0])

    def step_d2l(g):
        wait_bytes(every.at[row_x(3), row_y(2), span(g)], r_x.at[g, 0, 2])

    def step_d2r(g):
        ref = every.at[row_x(1), row_y(2), span(g)]
        wait_bytes(ref, r_x.at[g, 1, 2])
        relay(ref, r_r.at[g, 2], left)

    def step_othl(g):
        ref = other.at[row_x(3), span(g)]
        wait_bytes(ref, r_ox.at[g, 0])
        if g % 2:
            relay(ref, r_ro.at[g], right)
        send_y(g, 3)

    def step_othr(g):
        ref = other.at[row_x(1), span(g)]
        wait_bytes(ref, r_ox.at[g, 1])
        if g % 2 == 0:
            relay(ref, r_ro.at[g], left)
        send_y(g, 1)

    def step_oth2(g):
        wait_bytes(other.at[row_x(2), span(g)], r_ro.at[g])
        send_y(g, 2)

    def step_dot(g):
        for d in (0, 2):
            wait_bytes(every.at[row_x(2), row_y(d), span(g)], r_r.at[g, d])
        for col in (0, 1, 3, 2):
            for d in (1, 3):
                wait_bytes(every.at[row_x(col), row_y(d), span(g)], r_y.at[g, col, d])

        for xx in range(NX):
            for yy in range(NY):
                value = every[xx, yy, g * CHUNK:(g + 1) * CHUNK].reshape(CHUNK * 4, Q)
                top = value.astype(BF16)
                rows = pl.ds((xx * NY + yy) * CHUNK * 4, CHUNK * 4)
                high[rows, :] = top
                low[rows, :] = (value - top.astype(F32)).astype(BF16)
        result = jnp.dot(high[...], w_high[...], preferred_element_type=F32)
        result += jnp.dot(high[...], w_low[...], preferred_element_type=F32)
        result += jnp.dot(low[...], w_high[...], preferred_element_type=F32)
        part[pl.ds(g * CHUNK_ROWS, CHUNK_ROWS)] = result.reshape(CHUNK_ROWS, 4, 128)

    steps = {
        "own": step_own, "oth": step_oth, "yown": step_yown, "ownL": step_ownl, "ownR": step_ownr,
        "d2L": step_d2l, "d2R": step_d2r, "othL": step_othl, "othR": step_othr, "oth2": step_oth2,
        "dot": step_dot,
    }
    for name, g in ORDER:
        if name == "far":
            send_far()
        elif name == "select":
            select_integrals()
        elif name == "place":
            place_rows()
        else:
            steps[name](g)

    def arm_of(t):
        return (0, 8) if t == 0 else ((t + 1) % 2, 7 - (t - 1) // 2)

    def target_z(t):
        arm, d = arm_of(t)
        return (z + (NZ - d if arm else d)) % NZ

    def sources(t):
        arm, d = arm_of(t)
        arms = (0, 1) if t == 15 else (arm,)
        return [(a, e) for a in arms for e in range(1, 8 if a else 9) if NEXT[e] == d]

    def receiver(t):
        arm, d = arm_of(t)
        hops = d - NEXT[d]
        return device((z + (NZ - hops if arm else hops)) % NZ, y, x, c)

    def holds_rows(t, half):
        return target_z(t) * 128 + half * 64 < PAIRS

    def gather(t, half, core, first, count, use):
        base = target_z(t) * 128 + half * 64 + core * 32 + first

        @pl.loop(0, count, unroll=8)
        def _(i):
            use(i, part[place[base // 128, base % 128 + i]])

    partner_core = device(z, y, x, 1 - c)
    partner_y = device(z, y + 1 - 2 * parity, x, c)

    def step_gather(t):
        @pl.when(holds_rows(t, 0))
        def _():
            for turn, half in enumerate((1 - parity, parity)):
                def put(i, row):
                    core_out[t, half, i] = row
                gather(t, half, 1 - c, 0, BLOCK, put)
                remote(
                    core_out.at[t, half], core_in.at[t, half], s_c, r_c.at[t, turn], partner_core
                ).start()

    def piece(i):
        return pl.ds(i * PIECE, PIECE)

    def step_core(t):
        @pl.when(holds_rows(t, 0))
        def _():
            wait_bytes(core_in.at[t, 1 - parity], r_c.at[t, 0])

        @pl.when(holds_rows(t, 1 - parity))
        def _():
            def put_out(i, row):
                y_out[t, i] = row + core_in[t, 1 - parity, i]
            gather(t, 1 - parity, c, 0, NARROW, put_out)
            for i in range(PIECES):
                remote(y_out.at[t, piece(i)], y_in.at[t, piece(i)], s_s, r_s.at[t, i], partner_y).start()

        @pl.when(holds_rows(t, 0))
        def _():
            wait_bytes(core_in.at[t, parity], r_c.at[t, 1])

            def put_keep(i, row):
                y_keep[t, i] = row + core_in[t, parity, i]
            gather(t, parity, c, 0, NARROW, put_keep)
            for half in range(2):
                def put_wide(i, row):
                    wide[t, half, i] = row + core_in[t, half, NARROW + i]
                gather(t, half, c, NARROW, WIDE, put_wide)

    def finish(value, first):
        row = lax.broadcasted_iota(jnp.int32, value.shape, 0) + (cd * BLOCK + first)
        return jnp.where(row < PAIRS, value, 0.0)

    def step_sum(t, i):
        rows = piece(i)

        @pl.when(holds_rows(t, parity))
        def _():
            wait_bytes(y_in.at[t, rows], r_s.at[t, i])
            value = y_keep[t, rows] + y_in[t, rows]
            for arm, d in sources(t):
                wait_bytes(sum_in.at[arm, d - 1, rows], r_sum.at[arm, d - 1, i])
                value = value + sum_in[arm, d - 1, rows]
            if t == 15:
                out[rows] = finish(value, i * PIECE)
                return
            arm, d = arm_of(t)
            sum_out[t, rows] = value
            remote(
                sum_out.at[t, rows], sum_in.at[arm, d - 1, rows], s_sum,
                r_sum.at[arm, d - 1, i], receiver(t),
            ).start()

    def step_wide(t):
        @pl.when(holds_rows(t, 0))
        def _():
            value = wide[t]
            for arm, d in sources(t):
                wait_bytes(wide_in.at[arm, d - 1], r_wide.at[arm, d - 1])
                value = value + wide_in[arm, d - 1]
            wide_out[t] = value
            if t == 15:
                remote(wide_out.at[15, 1 - parity], y_last, s_last, r_last, partner_y).start()
                return
            arm, d = arm_of(t)
            remote(
                wide_out.at[t], wide_in.at[arm, d - 1], s_wide, r_wide.at[arm, d - 1], receiver(t)
            ).start()

    @pl.when(cd * BLOCK >= PAIRS)
    def _():
        out[...] = jnp.zeros(out.shape, F32)

    for name, t, i in SUMS:
        if name == "gather":
            step_gather(t)
        elif name == "core":
            step_core(t)
        elif name == "sum":
            step_sum(t, i)
        else:
            step_wide(t)

    @pl.when(holds_rows(15, 0))
    def _():
        wait_bytes(y_last, r_last)
        out[NARROW:BLOCK] = finish(wide_out[15, parity] + y_last[...], NARROW)

    wait_bytes(every.at[0, 0, pl.ds(0, 31)], s_z)
    wait_bytes(every.at[0, 0, pl.ds(0, 31)], s_z)
    for sem, units in ((s_w, 1), (s_y, 8), (s_x, 6), (s_r, 3)):
        for _ in range(units):
            wait_bytes(every.at[0, 0], sem)
    for t in range(16):
        @pl.when(holds_rows(t, 0))
        def _():
            wait_bytes(core_in.at[t], s_c)
            wait_bytes(wide_out.at[t] if t < 15 else y_last, s_wide if t < 15 else s_last)

        @pl.when(holds_rows(t, 1 - parity))
        def _():
            wait_bytes(y_in.at[t], s_s)

        if t < 15:
            @pl.when(holds_rows(t, parity))
            def _():
                wait_bytes(sum_out.at[t], s_sum)


def on_device(amplitudes, integrals, orbital_irrep, bra_pairs, ket_pairs, slot_pair):
    dma = pltpu.SemaphoreType.DMA
    result = pl.pallas_call(
        kernel,
        out_shape=jax.ShapeDtypeStruct((BLOCK, 4, 128), F32),
        in_specs=[
            pl.BlockSpec(memory_space=pl.ANY),
            pl.BlockSpec(memory_space=pl.ANY),
            pl.BlockSpec(memory_space=pltpu.VMEM),
            pl.BlockSpec(memory_space=pltpu.VMEM),
            pl.BlockSpec(memory_space=pltpu.VMEM),
            pl.BlockSpec(memory_space=pltpu.VMEM),
        ],
        out_specs=pl.BlockSpec(memory_space=pltpu.VMEM),
        scratch_shapes=[
            pltpu.VMEM((NX, NY, SLAB, 4, Q), F32),
            pltpu.VMEM((NX, SLAB, 4, Q), F32),
            pltpu.VMEM((CHUNK_ROWS, Q), BF16),
            pltpu.VMEM((CHUNK_ROWS, Q), BF16),
            pltpu.VMEM((Q, N), BF16),
            pltpu.VMEM((Q, N), BF16),
            pltpu.VMEM((N, Q), F32),
            pltpu.VMEM((SLOTS, 4, 128), F32),
            pltpu.VMEM((16, 128), jnp.int32),
            pltpu.SMEM((16, 128), jnp.int32),
            pltpu.VMEM((16, 2, BLOCK, 4, 128), F32),
            pltpu.VMEM((16, 2, BLOCK, 4, 128), F32),
            pltpu.VMEM((16, NARROW, 4, 128), F32),
            pltpu.VMEM((16, NARROW, 4, 128), F32),
            pltpu.VMEM((16, NARROW, 4, 128), F32),
            pltpu.VMEM((max(WIDE, 1), 4, 128), F32),
            pltpu.VMEM((16, 2, max(WIDE, 1), 4, 128), F32),
            pltpu.VMEM((16, NARROW, 4, 128), F32),
            pltpu.VMEM((2, 8, NARROW, 4, 128), F32),
            pltpu.VMEM((16, 2, max(WIDE, 1), 4, 128), F32),
            pltpu.VMEM((2, 8, 2, max(WIDE, 1), 4, 128), F32),
            pltpu.VMEM((4, NZ * 2048), F32), dma,
            pltpu.SemaphoreType.REGULAR, pltpu.SemaphoreType.REGULAR,
            dma, dma,
            dma, dma((CHUNKS,)), dma((CHUNKS,)),
            dma, dma, dma((CHUNKS, 4, 4)),
            dma, dma((CHUNKS, 2, 4)), dma((CHUNKS, 2)),
            dma, dma((CHUNKS, 4)), dma((CHUNKS,)),
            dma, dma((16, 2)),
            dma, dma((16, PIECES)),
            dma, dma((2, 8, PIECES)),
            dma, dma((2, 8)),
            dma, dma,
        ],
        compiler_params=pltpu.CompilerParams(
            collective_id=0, has_side_effects=True, vmem_limit_bytes=60 << 20
        ),
        name="ladder",
    )(amplitudes, integrals, orbital_irrep, bra_pairs, ket_pairs, slot_pair.reshape(16, 128))
    return result.reshape(BLOCK, N)


def solution(mesh):
    in_specs = (P(("cd", "ab"), None), P("ab", "cd"), P(), P(None, "ab"), P(None, "cd"), P())
    out_specs = P("cd", "ab")
    return jax.shard_map(
        on_device, mesh=mesh, in_specs=in_specs, out_specs=out_specs, check_vma=False
    )
```
